256 devices in a mesh: row: 16 (over x_hi, z), col: 16 (over y, x_lo, core).
Axes of the slice: x: 4 (x_hi: 2, x_lo: 2; x = x_hi * 2 + x_lo), y: 4, z: 8, core: 2. Of those that a mesh axis runs over, the one named last changes fastest.
Arguments:
- root_cot: bfloat16 [32, 32768], P(None, ('col', 'row')), may hold values from -6 to 6
- root_exercise: int32 [32, 32768], P(None, ('col', 'row')), may hold values 0 or 1
- mid_exercise: int32 [32, 32768], P(None, 'row'), may hold values 0 or 1
- mid_payoff: float32 [32, 32768], P(None, 'row'), may hold values from -6 to 6
- end_values: bfloat16 [32, 32768], P(None, ('col', 'row')), may hold values from -6 to 6
- root_points: float32 [4, 32768], P(None, ('col', 'row')), may hold values from -6 to 6
- mid_points: float32 [4, 32768], P(None, 'row'), may hold values from -6 to 6
- end_points: float32 [4, 32768], P(None, ('col', 'row')), may hold values from -6 to 6
- mid_weights: float32 [32768], P('row'), may hold values from 0.011048543 to 0.110485435
- end_weights: float32 [32768], P(('col', 'row')), may hold values from 0.011048543 to 0.110485435
- drift_rate: float32 [4], replicated, may hold values from 0.5 to 1
Outputs:
- terminal_cot: float32 [32, 32768], P(None, ('col', 'row'))
- grad_root: float32 [4, 32768], P(None, ('col', 'row'))
- grad_mid: float32 [4, 32768], P(None, ('row', 'col'))
- grad_end: float32 [4, 32768], P(None, ('col', 'row'))
The draws below stay inside these ranges and needn't reach their ends.
All inputs are finite; a program needn't handle non-finite values. No bound on the sum of `root_exercise` or of `mid_exercise` on one device may be relied on, other than what follows from the above.
Results may differ from the reference program's by a relative error of at most 0.012.
The reference program's roundings to bfloat16 on the way count: a program that leaves them out, or rounds other values in their place, can miss the bound.
Values may be sent and summed in bfloat16 or wider, within the bound.
No kernel may reach another device: no remote copies, remote signals or barrier semaphores. Data moves between devices by JAX's collectives and lax.ppermute only.
A program may use at most 64 MiB of HBM per device.

```python
import math
import jax
import jax.numpy as jnp
from jax import lax

PAY = 32
FACTORS = 4
NPTS = 32768


def draw_root_points(key, part):
    key = jax.random.fold_in(key, 11)
    return jnp.clip(3.0 * jax.random.normal(key, (FACTORS, NPTS), jnp.float32), -6.0, 6.0)


def draw_mid_points(key, part):
    key = jax.random.fold_in(key, 23)
    return jnp.clip(3.0 * jax.random.normal(key, (FACTORS, NPTS), jnp.float32), -6.0, 6.0)


def draw_end_points(key, part):
    key = jax.random.fold_in(key, 37)
    return jnp.clip(3.0 * jax.random.normal(key, (FACTORS, NPTS), jnp.float32), -6.0, 6.0)


def plant(result, key, low, high):
    spot = [jax.random.randint(jax.random.fold_in(key, axis), (), 0, length) for axis, length in enumerate(result.shape)]
    longest = result.shape.index(max(result.shape))
    beside = spot[:longest] + [(spot[longest] + 1) % result.shape[longest]] + spot[longest + 1:]
    return result.at[tuple(spot)].set(low).at[tuple(beside)].set(high)


def shard_levels(key, dims, split, smallest, largest):
    gain, own = 1.0, jax.random.fold_in(key, 6)
    for position, blocks in split:
        steps = jnp.exp(jax.random.uniform(jax.random.fold_in(own, position), (blocks,), jnp.float32, smallest / len(split), largest / len(split)))
        gain = gain * jnp.repeat(steps, dims[position] // blocks).reshape([-1 if axis == position else 1 for axis in range(len(dims))])
    return gain


def normal_values(own_key, extent, spread, reach, shards=(), held_as=jnp.bfloat16):
    loudness = shard_levels(own_key, extent, shards, -0.22, 0.18) if shards else 1.0
    values = jax.random.normal(own_key, extent, jnp.float32) * spread * loudness
    return jnp.minimum(jnp.maximum(values, -reach), reach).astype(held_as)


def setup_inputs(seed: int = 0) -> dict:
    key_list = jax.random.split(jax.random.key(seed), 12)
    return {
        "root_cot": normal_values(key_list[0], (PAY, NPTS), 1.0, 6.0, ((1, 256),)),
        "root_exercise": plant((jax.random.randint(key_list[1], (PAY, NPTS), 0, 3) < 1).astype(jnp.int32), jax.random.fold_in(key_list[1], 1), 0, 1),
        "mid_exercise": plant((jax.random.randint(key_list[2], (PAY, NPTS), 0, 3) < 1).astype(jnp.int32), jax.random.fold_in(key_list[2], 1), 0, 1),
        "mid_payoff": normal_values(key_list[3], (PAY, NPTS), 1.0, 6.0, ((1, 16),), jnp.float32),
        "end_values": normal_values(key_list[4], (PAY, NPTS), 1.0, 6.0, ((1, 256),)),
        "root_points": draw_root_points(jax.random.fold_in(key_list[11], 71), 0),
        "mid_points": draw_mid_points(jax.random.fold_in(key_list[11], 71), 0),
        "end_points": draw_end_points(jax.random.fold_in(key_list[11], 71), 0),
        "mid_weights": jnp.clip(jnp.exp(math.log(0.110485435) - 2.3025851 * jax.random.uniform(key_list[8], (NPTS,), jnp.float32) ** shard_levels(key_list[8], (NPTS,), ((0, 16),), -0.2, 0.2)), 0.011048543, 0.110485435),
        "end_weights": jnp.clip(jnp.exp(math.log(0.110485435) - 2.3025851 * jax.random.uniform(key_list[9], (NPTS,), jnp.float32) ** shard_levels(key_list[9], (NPTS,), ((0, 256),), -0.2, 0.2)), 0.011048543, 0.110485435),
        "drift_rate": jnp.clip(jnp.exp(jax.random.uniform(key_list[10], (FACTORS,), jnp.float32, math.log(0.5), math.log(1.0))), 0.5, 1.0),
    }


def kernel_tile(current, nexts, weights, drift_rate):
    shifted = drift_rate[:, None] * current
    distance = jnp.zeros((current.shape[1], nexts.shape[1]), jnp.float32)
    for factor in range(current.shape[0]):
        gap_vals = nexts[factor][None, :] - shifted[factor][:, None]
        distance = distance + gap_vals * gap_vals
    return weights[None, :] * jnp.exp(-0.5 * distance)

def with_ones(points):
    return jnp.concatenate([points.astype(jnp.bfloat16), jnp.ones((1, points.shape[1]), jnp.bfloat16)], axis=0)

def split_rows(array, height):
    return array.reshape(array.shape[0], -1, height).transpose(1, 0, 2)

def join_rows(stacked):
    return stacked.transpose(1, 0, 2).reshape(stacked.shape[1], -1)

def height_of(count):
    return count if count <= 512 else 512

def forward_tile(current, nexts, weights, next_values, drift_rate):
    height = height_of(current.shape[1])

    def visit(carry, block_pts):
        trans_b = kernel_tile(block_pts, nexts, weights, drift_rate).astype(jnp.bfloat16)
        cont = lax.dot_general(next_values, trans_b, (((1,), (1,)), ((), ())), preferred_element_type=jnp.float32)
        return (carry, cont)
    unused, blocks = lax.scan(visit, jnp.zeros((), jnp.float32), split_rows(current, height))
    return join_rows(blocks)

def backward_tile(current, nexts, weights, current_cot, next_values, drift_rate):
    height = height_of(current.shape[1])
    factors = current.shape[0]
    next_aug = with_ones(nexts)
    current_aug = with_ones(current)

    def visit(carry, item):
        next_cot, next_side = carry
        block_pts, block_aug, block_cot = item
        trans = kernel_tile(block_pts, nexts, weights, drift_rate)
        trans_b = trans.astype(jnp.bfloat16)
        next_cot = next_cot + jnp.dot(block_cot, trans_b, preferred_element_type=jnp.float32)
        weight_cot = lax.dot_general(block_cot, next_values, (((0,), (0,)), ((), ())), preferred_element_type=jnp.float32)
        scaled = (weight_cot * trans).astype(jnp.bfloat16)
        own_side = lax.dot_general(next_aug, scaled, (((1,), (1,)), ((), ())), preferred_element_type=jnp.float32)
        next_side = next_side + jnp.dot(block_aug, scaled, preferred_element_type=jnp.float32)
        grad_block = drift_rate[:, None] * (own_side[:factors] - drift_rate[:, None] * block_pts * own_side[factors:])
        return ((next_cot, next_side), grad_block)
    count = nexts.shape[1]
    init = (jnp.zeros((current_cot.shape[0], count), jnp.float32), jnp.zeros((factors + 1, count), jnp.float32))
    items = (split_rows(current, height), split_rows(current_aug, height), split_rows(current_cot, height))
    (next_cot, next_side), grads = lax.scan(visit, init, items)
    return (next_cot, join_rows(grads), next_side)

def side_grad(points, side, drift_rate):
    factors = points.shape[0]
    return -(points * side[factors:] - drift_rate[:, None] * side[:factors])

def reference(root_cot, root_exercise, mid_exercise, mid_payoff, end_values, root_points, mid_points, end_points, mid_weights, end_weights, drift_rate):
    mid_cont = forward_tile(mid_points, end_points, end_weights, end_values, drift_rate)
    mid_mask = mid_exercise.astype(jnp.float32)
    mid_values = (mid_mask * mid_payoff + (1.0 - mid_mask) * mid_cont).astype(jnp.bfloat16)
    root_dc = root_cot * (1 - root_exercise).astype(jnp.bfloat16)
    mid_cot, grad_root, mid_side = backward_tile(root_points, mid_points, mid_weights, root_dc, mid_values, drift_rate)
    mid_dc = ((1.0 - mid_mask) * mid_cot).astype(jnp.bfloat16)
    terminal_cot, mid_own, end_side = backward_tile(mid_points, end_points, end_weights, mid_dc, end_values, drift_rate)
    grad_mid = mid_own + side_grad(mid_points, mid_side, drift_rate)
    grad_end = side_grad(end_points, end_side, drift_rate)
    return (terminal_cot, grad_root, grad_mid, grad_end)
```

```python
import functools

import jax
import jax.numpy as jnp
from jax import lax
from jax.experimental import pallas as pl
from jax.experimental.pallas import tpu as pltpu
from jax.sharding import PartitionSpec as P

BF = jnp.bfloat16
F32 = jnp.float32
LANES = 128
PAY = 32
FACTORS = 4
SIDES = FACTORS + 1
HALF = 48
DEPTH = 32
WIDE = 256
DEEP = 2048
LIMIT = 56 * 1024 * 1024


def split3(value):
    high = value.astype(BF).astype(F32)
    rest = value - high
    middle = rest.astype(BF).astype(F32)
    return high, middle, (rest - middle).astype(BF).astype(F32)


def row_of(drift_ref, points):
    rows = lax.broadcasted_iota(jnp.int32, points.shape, 0)
    out = jnp.zeros(points.shape, F32)
    for factor in range(FACTORS):
        out = jnp.where(rows == factor, drift_ref[factor], out)
    return out


def square_sum(points):
    return jnp.sum(points * points, axis=0, keepdims=True)


def pack_kernel(cot_ref, exercise_ref, values_ref, root_ref, end_ref, weight_ref, drift_ref, out_ref, held):
    mask = 1.0 - exercise_ref[...].astype(F32)
    root = root_ref[...]
    end = end_ref[...]
    shifted = row_of(drift_ref, root) * root
    norms = (-0.5 * square_sum(end) + jnp.log(weight_ref[...]), -0.5 * square_sum(shifted))
    values = (values_ref[...].astype(F32), cot_ref[...].astype(F32) * mask)
    for half, (points, norm, pays) in enumerate(zip((end, root), norms, values)):
        base = HALF * half
        held[base : base + PAY, :] = pays
        for part, piece in enumerate(split3(points)):
            start = base + PAY + FACTORS * part
            held[start : start + FACTORS, :] = piece
        for part, piece in enumerate(split3(norm)):
            start = base + PAY + 3 * FACTORS + part
            held[start : start + 1, :] = piece
        held[base + HALF - 1 : base + HALF, :] = jnp.ones((1, LANES), F32)
    packed = held[...].astype(BF)
    for device in range(out_ref.shape[0]):
        out_ref[device] = packed


def far_factor(block):
    rows = lax.broadcasted_iota(jnp.int32, (8, block.shape[1]), 0)
    last = jnp.where(rows < FACTORS, block[0:8], jnp.where(rows < FACTORS + 2, 1.0, 0.0))
    return jnp.concatenate([block[0:8], block[0:8], block[8:16], last], axis=0)


def near_factor(points, norm, drift, held):
    high, middle, low = split3(drift * points)
    norms = split3(norm)
    ones = jnp.ones((3, points.shape[1]), F32)
    held[0:4, :] = high
    held[4:8, :] = high
    held[8:12, :] = middle
    held[12:16, :] = middle
    held[16:20, :] = high
    held[20:23, :] = ones
    held[23:24, :] = norms[0]
    held[24:28, :] = low
    held[28:29, :] = norms[1]
    held[29:30, :] = norms[2]
    held[30:32, :] = jnp.zeros((2, points.shape[1]), F32)


def near_norms(points, weights, drift):
    shifted = drift * points
    return (-0.5 * square_sum(shifted), -0.5 * square_sum(points) + jnp.log(weights))


def sums_tile(weights_ref, left_ref, right, deep):
    total = None
    for start in range(0, left_ref.shape[0], deep):
        power = jnp.dot(left_ref[start : start + deep, :], right, preferred_element_type=F32)
        trans = jnp.exp(power).astype(BF)
        part = jnp.dot(weights_ref[:, start : start + deep], trans, preferred_element_type=F32)
        total = part if total is None else total + part
    return total


def first_kernel(wide, deep, gathered_ref, points_ref, weights_ref, drift_ref, sent_ref, sums_ref, held, near, far, scaled):
    points = points_ref[...]
    drift = row_of(drift_ref, points)
    norms = near_norms(points, weights_ref[...], drift)
    for half in range(2):
        near_factor(points, norms[half], drift, held)
        near[half] = held[...].astype(BF)
        for chunk in range(gathered_ref.shape[0]):
            columns = slice(chunk * LANES, (chunk + 1) * LANES)
            block = gathered_ref[chunk, HALF * half : HALF * (half + 1), :].astype(F32)
            pays, packed = block[:PAY], block[PAY:]
            far[half, columns, :] = far_factor(packed).T.astype(BF)
            for factor in range(FACTORS):
                scaled[half, PAY * factor : PAY * (factor + 1), columns] = (
                    pays * packed[factor : factor + 1]
                ).astype(BF)
            scaled[half, PAY * FACTORS :, columns] = pays.astype(BF)
    for half in range(2):

        def visit(tile, carry, half=half):
            columns = pl.ds(pl.multiple_of(tile * wide, wide), wide)
            total = sums_tile(scaled.at[half], far.at[half], near[half, :, columns], deep)
            sums_ref[half, :, columns] = total
            last = total[PAY * FACTORS :].astype(BF)
            for piece in range(wide // LANES):
                sent_ref[tile * (wide // LANES) + piece, PAY * half : PAY * (half + 1), :] = last[
                    :, piece * LANES : (piece + 1) * LANES
                ]
            return carry

        lax.fori_loop(0, points.shape[1] // wide, visit, 0)


def middle_kernel(index_ref, got_ref, exercise_ref, payoff_ref, out_ref):
    total = got_ref[0].astype(F32)
    for device in range(1, got_ref.shape[0]):
        total = total + got_ref[device].astype(F32)
    mask = exercise_ref[...].astype(F32)
    values = mask * payoff_ref[...] + (1.0 - mask) * total[:PAY]
    cots = (1.0 - mask) * total[PAY:]
    packed = jnp.concatenate([values, cots], axis=0).astype(BF)
    for device in range(out_ref.shape[0]):
        out_ref[device] = packed


def weighted(pays, sums):
    return [
        jnp.sum(pays * sums[PAY * side : PAY * (side + 1)], axis=0, keepdims=True)
        for side in range(SIDES)
    ]


def second_kernel(
    wide, deep, middle_ref, gathered_ref, points_ref, weights_ref, drift_ref, sums_ref,
    sent_ref, own_ref, held, near, far, scaled,
):
    points = points_ref[...]
    drift = row_of(drift_ref, points)
    norms = near_norms(points, weights_ref[...], drift)
    rounded = points.astype(BF).astype(F32)
    chunks = middle_ref.shape[0]
    for half in range(2):
        near_factor(points, norms[half], drift, held)
        near[half] = held[...].T.astype(BF)
        rows = slice(PAY * (1 - half), PAY * (2 - half))
        for chunk in range(chunks):
            columns = slice(chunk * LANES, (chunk + 1) * LANES)
            far[half, :, columns] = far_factor(
                gathered_ref[chunk, HALF * half + PAY : HALF * (half + 1), :].astype(F32)
            ).astype(BF)
            pays = middle_ref[chunk, rows, :].astype(F32)
            for factor in range(FACTORS):
                scaled[half, PAY * factor : PAY * (factor + 1), columns] = (
                    pays * rounded[factor : factor + 1, columns]
                ).astype(BF)
            scaled[half, PAY * FACTORS :, columns] = pays.astype(BF)
    for chunk in range(chunks):
        columns = slice(chunk * LANES, (chunk + 1) * LANES)
        after = weighted(middle_ref[chunk, PAY:, :].astype(F32), sums_ref[0, :, columns])
        before = weighted(middle_ref[chunk, :PAY, :].astype(F32), sums_ref[1, :, columns])
        for factor in range(FACTORS):
            rate = drift_ref[factor]
            place = points[factor : factor + 1, columns]
            own_ref[chunk, factor : factor + 1, :] = rate * (
                after[factor] - rate * place * after[FACTORS]
            ) - (place * before[FACTORS] - rate * before[factor])
    for half in range(2):

        def visit(tile, carry, half=half):
            columns = pl.ds(pl.multiple_of(tile * wide, wide), wide)
            total = sums_tile(scaled.at[half], near.at[half], far[half, :, columns], deep)
            for piece in range(wide // LANES):
                chunk = tile * (wide // LANES) + piece
                part = total[:, piece * LANES : (piece + 1) * LANES]
                block = gathered_ref[chunk, HALF * half : HALF * (half + 1), :].astype(F32)
                sides = weighted(block[:PAY], part)
                place = block[PAY : PAY + 4] + block[PAY + 4 : PAY + 8] + block[PAY + 8 : PAY + 12]
                grads = []
                for factor in range(FACTORS):
                    rate = drift_ref[factor]
                    spot = place[factor : factor + 1]
                    if half == 0:
                        grads.append(rate * sides[factor] - spot * sides[FACTORS])
                    else:
                        grads.append(rate * (sides[factor] - rate * spot * sides[FACTORS]))
                if half == 0:
                    sent_ref[chunk, 0:PAY, :] = part[PAY * FACTORS :].astype(BF)
                held[PAY * 0 + 8 * half : 8 * half + 4, 0:LANES] = jnp.concatenate(grads, axis=0)
                held[8 * half + 4 : 8 * half + 8, 0:LANES] = jnp.zeros((4, LANES), F32)
                sent_ref[chunk, PAY + 8 * half : PAY + 8 * half + 8, :] = held[
                    8 * half : 8 * half + 8, 0:LANES
                ].astype(BF)
            return carry

        lax.fori_loop(0, chunks * LANES // wide, visit, 0)


def last_kernel(got_ref, own_ref, terminal_ref, root_ref, mid_ref, end_ref):
    total = got_ref[0].astype(F32)
    own = own_ref[0]
    for device in range(1, got_ref.shape[0]):
        total = total + got_ref[device].astype(F32)
        own = own + own_ref[device]
    terminal_ref[...] = total[:PAY]
    end_ref[...] = total[PAY : PAY + FACTORS]
    root_ref[...] = total[PAY + 8 : PAY + 8 + FACTORS]
    mid_ref[...] = own


VMEM = pl.BlockSpec(memory_space=pltpu.VMEM)
SMEM = pl.BlockSpec(memory_space=pltpu.SMEM)
PARAMS = pltpu.CompilerParams(vmem_limit_bytes=LIMIT)


def shape(dims, dtype):
    return jax.ShapeDtypeStruct(dims, dtype)


def pack_call(count, cot, exercise, values, root, end, weights, drift):
    return pl.pallas_call(
        pack_kernel,
        out_shape=shape((count, 2 * HALF, LANES), BF),
        in_specs=[VMEM] * 6 + [SMEM],
        out_specs=VMEM,
        scratch_shapes=[pltpu.VMEM((2 * HALF, LANES), F32)],
        compiler_params=PARAMS,
    )(cot, exercise, values, root, end, weights, drift)


def first_call(gathered, points, weights, drift, wide=WIDE, deep=DEEP):
    count, size = gathered.shape[0], points.shape[1]
    return pl.pallas_call(
        functools.partial(first_kernel, wide, deep),
        out_shape=(shape((size // LANES, 2 * PAY, LANES), BF), shape((2, SIDES * PAY, size), F32)),
        in_specs=[VMEM] * 3 + [SMEM],
        out_specs=(VMEM, VMEM),
        scratch_shapes=[
            pltpu.VMEM((DEPTH, size), F32),
            pltpu.VMEM((2, DEPTH, size), BF),
            pltpu.VMEM((2, count * LANES, DEPTH), BF),
            pltpu.VMEM((2, SIDES * PAY, count * LANES), BF),
        ],
        compiler_params=PARAMS,
    )(gathered, points, weights, drift)


def middle_call(index, got, exercise, payoff):
    count = got.shape[0]
    return pl.pallas_call(
        middle_kernel,
        out_shape=shape((count, 2 * PAY, LANES), BF),
        grid_spec=pltpu.PrefetchScalarGridSpec(
            num_scalar_prefetch=1,
            grid=(1,),
            in_specs=[
                pl.BlockSpec((count, 2 * PAY, LANES), lambda step, place: (0, 0, 0)),
                pl.BlockSpec((PAY, LANES), lambda step, place: (0, place[0])),
                pl.BlockSpec((PAY, LANES), lambda step, place: (0, place[0])),
            ],
            out_specs=pl.BlockSpec((count, 2 * PAY, LANES), lambda step, place: (0, 0, 0)),
        ),
        compiler_params=PARAMS,
    )(index, got, exercise, payoff)


def second_call(middle, gathered, points, weights, drift, sums, wide=WIDE, deep=DEEP):
    count, size = gathered.shape[0], points.shape[1]
    return pl.pallas_call(
        functools.partial(second_kernel, wide, deep),
        out_shape=(
            shape((count, HALF, LANES), BF),
            shape((size // LANES, FACTORS, LANES), F32),
        ),
        in_specs=[VMEM] * 4 + [SMEM, VMEM],
        out_specs=(VMEM, VMEM),
        scratch_shapes=[
            pltpu.VMEM((DEPTH, size), F32),
            pltpu.VMEM((2, size, DEPTH), BF),
            pltpu.VMEM((2, DEPTH, count * LANES), BF),
            pltpu.VMEM((2, SIDES * PAY, size), BF),
        ],
        compiler_params=PARAMS,
    )(middle, gathered, points, weights, drift, sums)


def last_call(got, own):
    return pl.pallas_call(
        last_kernel,
        out_shape=(shape((PAY, LANES), F32),) + (shape((FACTORS, LANES), F32),) * 3,
        in_specs=[VMEM] * 2,
        out_specs=(VMEM,) * 4,
        compiler_params=PARAMS,
    )(got, own)


def on_device(
    root_cot,
    root_exercise,
    mid_exercise,
    mid_payoff,
    end_values,
    root_points,
    mid_points,
    end_points,
    mid_weights,
    end_weights,
    drift_rate,
):
    rows = lax.axis_size("row")
    weights = mid_weights[None, :]
    packed = pack_call(
        rows, root_cot, root_exercise, end_values, root_points, end_points, end_weights[None, :], drift_rate
    )
    gathered = lax.all_to_all(packed, "row", 0, 0)
    parts, sums = first_call(gathered, mid_points, weights, drift_rate)
    got = lax.all_to_all(parts, "col", 0, 0)
    index = lax.axis_index("col")[None]
    values = middle_call(index, got, mid_exercise, mid_payoff)
    middle = lax.all_to_all(values, "col", 0, 0)
    far, own = second_call(middle, gathered, mid_points, weights, drift_rate, sums)
    own = lax.all_to_all(own, "col", 0, 0)
    far = lax.all_to_all(far, "row", 0, 0)
    terminal, grad_root, grad_mid, grad_end = last_call(far, own)
    return (terminal, grad_root, grad_mid, grad_end)


def solution(mesh):
    in_specs = (
        P(None, ("col", "row")),
        P(None, ("col", "row")),
        P(None, "row"),
        P(None, "row"),
        P(None, ("col", "row")),
        P(None, ("col", "row")),
        P(None, "row"),
        P(None, ("col", "row")),
        P("row"),
        P(("col", "row")),
        P(),
    )
    out_specs = (
        P(None, ("col", "row")),
        P(None, ("col", "row")),
        P(None, ("row", "col")),
        P(None, ("col", "row")),
    )
    return jax.shard_map(
        on_device, mesh=mesh, in_specs=in_specs, out_specs=out_specs, check_vma=False
    )
```

```python
import functools

import jax
import jax.numpy as jnp
from jax import lax
from jax.experimental import pallas as pl
from jax.experimental.pallas import tpu as pltpu
from jax.sharding import PartitionSpec as P

BF = jnp.bfloat16
F32 = jnp.float32
LANES = 128
PAY = 32
FACTORS = 4
SIDES = FACTORS + 1
HALF = 48
DEPTH = 32
DEEP = 256
LIMIT = 36 * 1024 * 1024


def split3(value):
    high = value.astype(BF).astype(F32)
    rest = value - high
    middle = rest.astype(BF).astype(F32)
    return high, middle, (rest - middle).astype(BF).astype(F32)


def row_of(drift_ref, points):
    rows = lax.broadcasted_iota(jnp.int32, points.shape, 0)
    out = jnp.zeros(points.shape, F32)
    for factor in range(FACTORS):
        out = jnp.where(rows == factor, drift_ref[factor], out)
    return out


def square_sum(points):
    return jnp.sum(points * points, axis=0, keepdims=True)


def fetch(sources, places, sems):
    copies = [
        pltpu.make_async_copy(source, place, sems.at[number])
        for number, (source, place) in enumerate(zip(sources, places))
    ]
    for copy in copies:
        copy.start()
    return copies


def arrive(copies):
    for copy in copies:
        copy.wait()


def pack_kernel(
    cot_hbm, exercise_hbm, values_hbm, root_hbm, end_hbm, weight_hbm, drift_hbm, out_ref,
    held, sems, cot_ref, exercise_ref, values_ref, root_ref, end_ref, weight_ref, drift_ref,
):
    arrive(
        fetch(
            (cot_hbm, exercise_hbm, values_hbm, root_hbm, end_hbm, weight_hbm, drift_hbm),
            (cot_ref, exercise_ref, values_ref, root_ref, end_ref, weight_ref, drift_ref),
            sems,
        )
    )
    mask = 1.0 - exercise_ref[...].astype(F32)
    root = root_ref[...]
    end = end_ref[...]
    shifted = row_of(drift_ref, root) * root
    norms = (-0.5 * square_sum(end) + jnp.log(weight_ref[...]), -0.5 * square_sum(shifted))
    values = (values_ref[...].astype(F32), cot_ref[...].astype(F32) * mask)
    for half, (points, norm, pays) in enumerate(zip((end, root), norms, values)):
        base = HALF * half
        held[base : base + PAY, :] = pays
        for part, piece in enumerate(split3(points)):
            start = base + PAY + FACTORS * part
            held[start : start + FACTORS, :] = piece
        for part, piece in enumerate(split3(norm)):
            start = base + PAY + 3 * FACTORS + part
            held[start : start + 1, :] = piece
        held[base + HALF - 1 : base + HALF, :] = jnp.ones((1, LANES), F32)
    packed = held[...].astype(BF)
    for device in range(out_ref.shape[0]):
        out_ref[device] = packed


def far_factor(block):
    rows = lax.broadcasted_iota(jnp.int32, (8, block.shape[1]), 0)
    last = jnp.where(rows < FACTORS, block[0:8], jnp.where(rows < FACTORS + 2, 1.0, 0.0))
    return jnp.concatenate([block[0:8], block[0:8], block[8:16], last], axis=0)


def near_factor(points, norm, drift, held):
    high, middle, low = split3(drift * points)
    norms = split3(norm)
    ones = jnp.ones((3, points.shape[1]), F32)
    held[0:4, :] = high
    held[4:8, :] = high
    held[8:12, :] = middle
    held[12:16, :] = middle
    held[16:20, :] = high
    held[20:23, :] = ones
    held[23:24, :] = norms[0]
    held[24:28, :] = low
    held[28:29, :] = norms[1]
    held[29:30, :] = norms[2]
    held[30:32, :] = jnp.zeros((2, points.shape[1]), F32)


def near_norms(points, weights, drift):
    shifted = drift * points
    return (-0.5 * square_sum(shifted), -0.5 * square_sum(points) + jnp.log(weights))


def first_kernel(
    deep, gathered_ref, points_hbm, weights_hbm, drift_hbm, sent_ref, sums_ref,
    held, near, far, scaled, sems, points_ref, weights_ref, drift_ref,
):
    arrivals = fetch((points_hbm, weights_hbm, drift_hbm), (points_ref, weights_ref, drift_ref), sems)
    chunks = gathered_ref.shape[0]
    for half in range(2):
        for chunk in range(chunks):
            columns = slice(chunk * LANES, (chunk + 1) * LANES)
            block = gathered_ref[chunk, HALF * half : HALF * (half + 1), :].astype(F32)
            pays, packed = block[:PAY], block[PAY:]
            far[half, columns, :] = far_factor(packed).T.astype(BF)
            for factor in range(FACTORS):
                scaled[half, PAY * factor : PAY * (factor + 1), columns] = (
                    pays * packed[factor : factor + 1]
                ).astype(BF)
            scaled[half, PAY * FACTORS :, columns] = pays.astype(BF)
    arrive(arrivals)
    points = points_ref[...]
    drift = row_of(drift_ref, points)
    norms = near_norms(points, weights_ref[...], drift)
    for half in range(2):
        near_factor(points, norms[half], drift, held)
        near[half] = held[...].astype(BF)
    for half in range(2):
        right = near[half]
        for start in range(0, chunks * LANES, deep):
            rows = slice(start, start + deep)
            power = jnp.dot(far[half, rows, :], right, preferred_element_type=F32)
            trans = jnp.exp(power).astype(BF)
            part = jnp.dot(scaled[half, :, rows], trans, preferred_element_type=F32)
            sums_ref[half] = part if start == 0 else sums_ref[half] + part
        last = sums_ref[half, PAY * FACTORS :, :].astype(BF)
        for chunk in range(sent_ref.shape[0]):
            sent_ref[chunk, PAY * half : PAY * (half + 1), :] = last[
                :, chunk * LANES : (chunk + 1) * LANES
            ]


def middle_kernel(index_ref, got_ref, exercise_hbm, payoff_hbm, out_ref, sems, exercise_ref, payoff_ref):
    columns = pl.ds(pl.multiple_of(index_ref[0] * LANES, LANES), LANES)
    arrivals = fetch(
        (exercise_hbm.at[:, columns], payoff_hbm.at[:, columns]), (exercise_ref, payoff_ref), sems
    )
    total = got_ref[0].astype(F32)
    for device in range(1, got_ref.shape[0]):
        total = total + got_ref[device].astype(F32)
    arrive(arrivals)
    mask = exercise_ref[...].astype(F32)
    values = mask * payoff_ref[...] + (1.0 - mask) * total[:PAY]
    cots = (1.0 - mask) * total[PAY:]
    packed = jnp.concatenate([values, cots], axis=0).astype(BF)
    for device in range(out_ref.shape[0]):
        out_ref[device] = packed


def weighted(pays, sums):
    return [
        jnp.sum(pays * sums[PAY * side : PAY * (side + 1)], axis=0, keepdims=True)
        for side in range(SIDES)
    ]


def own_kernel(middle_ref, points_hbm, drift_hbm, sums_ref, far_hbm, own_ref, sems, points_ref, drift_ref):
    arrive(fetch((points_hbm, drift_hbm), (points_ref, drift_ref), sems))
    for chunk in range(middle_ref.shape[0]):
        columns = slice(chunk * LANES, (chunk + 1) * LANES)
        after = weighted(middle_ref[chunk, PAY:, :].astype(F32), sums_ref[0, :, columns])
        before = weighted(middle_ref[chunk, :PAY, :].astype(F32), sums_ref[1, :, columns])
        for factor in range(FACTORS):
            rate = drift_ref[factor]
            place = points_ref[factor : factor + 1, columns]
            own_ref[chunk, factor : factor + 1, :] = rate * (
                after[factor] - rate * place * after[FACTORS]
            ) - (place * before[FACTORS] - rate * before[factor])


def second_kernel(
    deep, middle_ref, gathered_ref, points_hbm, weights_hbm, drift_hbm, sent_ref,
    held, total, near, far, scaled, sems, points_ref, weights_ref, drift_ref,
):
    arrivals = fetch((points_hbm, weights_hbm, drift_hbm), (points_ref, weights_ref, drift_ref), sems)
    chunks = middle_ref.shape[0]
    for half in range(2):
        for chunk in range(chunks):
            columns = slice(chunk * LANES, (chunk + 1) * LANES)
            far[half, :, columns] = far_factor(
                gathered_ref[chunk, HALF * half + PAY : HALF * (half + 1), :].astype(F32)
            ).astype(BF)
    arrive(arrivals)
    points = points_ref[...]
    rounded = points.astype(BF).astype(F32)
    drift = row_of(drift_ref, points)
    norms = near_norms(points, weights_ref[...], drift)
    for half in range(2):
        near_factor(points, norms[half], drift, held)
        near[half] = held[...].T.astype(BF)
        rows = slice(PAY * (1 - half), PAY * (2 - half))
        for chunk in range(chunks):
            columns = slice(chunk * LANES, (chunk + 1) * LANES)
            pays = middle_ref[chunk, rows, :].astype(F32)
            for factor in range(FACTORS):
                scaled[half, PAY * factor : PAY * (factor + 1), columns] = (
                    pays * rounded[factor : factor + 1, columns]
                ).astype(BF)
            scaled[half, PAY * FACTORS :, columns] = pays.astype(BF)
    for half in range(2):
        right = far[half]
        for start in range(0, points.shape[1], deep):
            rows = slice(start, start + deep)
            power = jnp.dot(near[half, rows, :], right, preferred_element_type=F32)
            trans = jnp.exp(power).astype(BF)
            part = jnp.dot(scaled[half, :, rows], trans, preferred_element_type=F32)
            total[half] = part if start == 0 else total[half] + part
        for chunk in range(chunks):
            part = total[half, :, chunk * LANES : (chunk + 1) * LANES]
            block = gathered_ref[chunk, HALF * half : HALF * (half + 1), :].astype(F32)
            sides = weighted(block[:PAY], part)
            place = block[PAY : PAY + 4] + block[PAY + 4 : PAY + 8] + block[PAY + 8 : PAY + 12]
            for factor in range(FACTORS):
                rate = drift_ref[factor]
                spot = place[factor : factor + 1]
                if half == 0:
                    grad = rate * sides[factor] - spot * sides[FACTORS]
                else:
                    grad = rate * (sides[factor] - rate * spot * sides[FACTORS])
                row = FACTORS * half + factor
                held[row : row + 1, chunk * LANES : (chunk + 1) * LANES] = grad
            if half == 0:
                sent_ref[chunk, 0:PAY, :] = part[PAY * FACTORS :].astype(BF)
    for chunk in range(chunks):
        sent_ref[chunk, PAY:, :] = held[0:16, chunk * LANES : (chunk + 1) * LANES].astype(BF)


def last_kernel(got_ref, own_ref, terminal_ref, root_ref, mid_ref, end_ref):
    total = got_ref[0].astype(F32)
    own = own_ref[0]
    for device in range(1, got_ref.shape[0]):
        total = total + got_ref[device].astype(F32)
        own = own + own_ref[device]
    terminal_ref[...] = total[:PAY]
    end_ref[...] = total[PAY : PAY + FACTORS]
    root_ref[...] = total[PAY + FACTORS : PAY + 2 * FACTORS]
    mid_ref[...] = own


VMEM = pl.BlockSpec(memory_space=pltpu.VMEM)
HBM = pl.BlockSpec(memory_space=pltpu.HBM)
SMEM = pl.BlockSpec(memory_space=pltpu.SMEM)
PARAMS = pltpu.CompilerParams(vmem_limit_bytes=LIMIT)


def shape(dims, dtype):
    return jax.ShapeDtypeStruct(dims, dtype)


def held_back(*arrays):
    return [pltpu.with_memory_space_constraint(array, pltpu.HBM) for array in arrays]


def staged(*arrays):
    blocks = [pltpu.VMEM(array.shape, array.dtype) for array in arrays[:-1]]
    return blocks + [pltpu.SMEM(arrays[-1].shape, arrays[-1].dtype)]


def pack_call(count, *arrays):
    return pl.pallas_call(
        pack_kernel,
        out_shape=shape((count, 2 * HALF, LANES), BF),
        in_specs=[HBM] * 7,
        out_specs=VMEM,
        scratch_shapes=[pltpu.VMEM((2 * HALF, LANES), F32), pltpu.SemaphoreType.DMA((7,))]
        + staged(*arrays),
        compiler_params=PARAMS,
    )(*held_back(*arrays))


def first_call(gathered, points, weights, drift):
    count, size = gathered.shape[0], points.shape[1]
    deep = DEEP
    return pl.pallas_call(
        functools.partial(first_kernel, deep),
        out_shape=(
            shape((size // LANES, 2 * PAY, LANES), BF),
            shape((2, SIDES * PAY, size), F32),
        ),
        in_specs=[VMEM] + [HBM] * 3,
        out_specs=(VMEM, VMEM),
        scratch_shapes=[
            pltpu.VMEM((DEPTH, size), F32),
            pltpu.VMEM((2, DEPTH, size), BF),
            pltpu.VMEM((2, count * LANES, DEPTH), BF),
            pltpu.VMEM((2, SIDES * PAY, count * LANES), BF),
            pltpu.SemaphoreType.DMA((3,)),
        ]
        + staged(points, weights, drift),
        compiler_params=PARAMS,
    )(gathered, *held_back(points, weights, drift))


def middle_call(index, got, exercise, payoff):
    return pl.pallas_call(
        middle_kernel,
        out_shape=shape(got.shape, BF),
        in_specs=[SMEM, VMEM, HBM, HBM],
        out_specs=VMEM,
        scratch_shapes=[
            pltpu.SemaphoreType.DMA((2,)),
            pltpu.VMEM((PAY, LANES), jnp.int32),
            pltpu.VMEM((PAY, LANES), F32),
        ],
        compiler_params=PARAMS,
    )(index, got, *held_back(exercise, payoff))


def own_call(middle, points, drift, sums, far):
    return pl.pallas_call(
        own_kernel,
        out_shape=shape((middle.shape[0], FACTORS, LANES), F32),
        in_specs=[VMEM, HBM, HBM, VMEM, HBM],
        out_specs=VMEM,
        scratch_shapes=[pltpu.SemaphoreType.DMA((2,))] + staged(points, drift),
        compiler_params=PARAMS,
    )(middle, *held_back(points, drift), sums, far)


def second_call(middle, gathered, points, weights, drift):
    count, size = gathered.shape[0], points.shape[1]
    return pl.pallas_call(
        functools.partial(second_kernel, DEEP),
        out_shape=shape((count, HALF, LANES), BF),
        in_specs=[VMEM] * 2 + [HBM] * 3,
        out_specs=VMEM,
        scratch_shapes=[
            pltpu.VMEM((DEPTH, size), F32),
            pltpu.VMEM((2, SIDES * PAY, count * LANES), F32),
            pltpu.VMEM((2, size, DEPTH), BF),
            pltpu.VMEM((2, DEPTH, count * LANES), BF),
            pltpu.VMEM((2, SIDES * PAY, size), BF),
            pltpu.SemaphoreType.DMA((3,)),
        ]
        + staged(points, weights, drift),
        compiler_params=PARAMS,
    )(middle, gathered, *held_back(points, weights, drift))


def last_call(got, own):
    return pl.pallas_call(
        last_kernel,
        out_shape=(shape((PAY, LANES), F32),) + (shape((FACTORS, LANES), F32),) * 3,
        in_specs=[VMEM] * 2,
        out_specs=(VMEM,) * 4,
        compiler_params=PARAMS,
    )(got, own)


def exchange(blocks, axis):
    return lax.all_to_all(blocks, axis, 0, 0)


def on_device(
    root_cot,
    root_exercise,
    mid_exercise,
    mid_payoff,
    end_values,
    root_points,
    mid_points,
    end_points,
    mid_weights,
    end_weights,
    drift_rate,
):
    rows = lax.axis_size("row")
    weights = mid_weights[None, :]
    packed = pack_call(
        rows, root_cot, root_exercise, end_values, root_points, end_points, end_weights[None, :], drift_rate
    )
    gathered = exchange(packed, "row")
    parts, sums = first_call(gathered, mid_points, weights, drift_rate)
    got = exchange(parts, "col")
    values = middle_call(lax.axis_index("col")[None], got, mid_exercise, mid_payoff)
    middle = exchange(values, "col")
    sides = second_call(middle, gathered, mid_points, weights, drift_rate)
    far = exchange(sides, "row")
    own = exchange(own_call(middle, mid_points, drift_rate, sums, sides), "col")
    terminal, grad_root, grad_mid, grad_end = last_call(far, own)
    return (terminal, grad_root, grad_mid, grad_end)


def solution(mesh):
    in_specs = (
        P(None, ("col", "row")),
        P(None, ("col", "row")),
        P(None, "row"),
        P(None, "row"),
        P(None, ("col", "row")),
        P(None, ("col", "row")),
        P(None, "row"),
        P(None, ("col", "row")),
        P("row"),
        P(("col", "row")),
        P(),
    )
    out_specs = (
        P(None, ("col", "row")),
        P(None, ("col", "row")),
        P(None, ("row", "col")),
        P(None, ("col", "row")),
    )
    return jax.shard_map(
        on_device, mesh=mesh, in_specs=in_specs, out_specs=out_specs, check_vma=False
    )
```

```python
import functools

import jax
import jax.numpy as jnp
from jax import lax
from jax.experimental import pallas as pl
from jax.experimental.pallas import tpu as pltpu
from jax.sharding import PartitionSpec as P

BF = jnp.bfloat16
F32 = jnp.float32
LANES = 128
PAY = 32
FACTORS = 4
SIDES = FACTORS + 1
HALF = 48
DEPTH = 32
DEEP = 256
PIECE = 512
BLOCK = 1024
AHEAD = 2
EARLY = 1024
LIMIT = 36 * 1024 * 1024


def split3(value):
    high = value.astype(BF).astype(F32)
    rest = value - high
    middle = rest.astype(BF).astype(F32)
    return high, middle, (rest - middle).astype(BF).astype(F32)


def row_of(drift_ref, points):
    rows = lax.broadcasted_iota(jnp.int32, points.shape, 0)
    out = jnp.zeros(points.shape, F32)
    for factor in range(FACTORS):
        out = jnp.where(rows == factor, drift_ref[factor], out)
    return out


def square_sum(points):
    return jnp.sum(points * points, axis=0, keepdims=True)


def fetch(sources, places, sems):
    copies = [
        pltpu.make_async_copy(source, place, sems.at[number])
        for number, (source, place) in enumerate(zip(sources, places))
    ]
    for copy in copies:
        copy.start()
    return copies


def arrive(copies):
    for copy in copies:
        copy.wait()


def pack_kernel(
    cot_hbm, exercise_hbm, values_hbm, root_hbm, end_hbm, weight_hbm, drift_hbm, out_ref,
    held, sems, cot_ref, exercise_ref, values_ref, root_ref, end_ref, weight_ref, drift_ref,
):
    arrive(
        fetch(
            (cot_hbm, exercise_hbm, values_hbm, root_hbm, end_hbm, weight_hbm, drift_hbm),
            (cot_ref, exercise_ref, values_ref, root_ref, end_ref, weight_ref, drift_ref),
            sems,
        )
    )
    mask = 1.0 - exercise_ref[...].astype(F32)
    root = root_ref[...]
    end = end_ref[...]
    shifted = row_of(drift_ref, root) * root
    norms = (-0.5 * square_sum(end) + jnp.log(weight_ref[...]), -0.5 * square_sum(shifted))
    values = (values_ref[...].astype(F32), cot_ref[...].astype(F32) * mask)
    for half, (points, norm, pays) in enumerate(zip((end, root), norms, values)):
        base = HALF * half
        held[base : base + PAY, :] = pays
        for part, piece in enumerate(split3(points)):
            start = base + PAY + FACTORS * part
            held[start : start + FACTORS, :] = piece
        for part, piece in enumerate(split3(norm)):
            start = base + PAY + 3 * FACTORS + part
            held[start : start + 1, :] = piece
        held[base + HALF - 1 : base + HALF, :] = jnp.ones((1, LANES), F32)
    packed = held[...].astype(BF)
    for device in range(out_ref.shape[0]):
        out_ref[device] = packed


def far_factor(block):
    rows = lax.broadcasted_iota(jnp.int32, (8, block.shape[1]), 0)
    last = jnp.where(rows < FACTORS, block[0:8], jnp.where(rows < FACTORS + 2, 1.0, 0.0))
    return jnp.concatenate([block[0:8], block[0:8], block[8:16], last], axis=0)


def near_factor(points, norm, drift, held):
    high, middle, low = split3(drift * points)
    norms = split3(norm)
    ones = jnp.ones((3, points.shape[1]), F32)
    held[0:4, :] = high
    held[4:8, :] = high
    held[8:12, :] = middle
    held[12:16, :] = middle
    held[16:20, :] = high
    held[20:23, :] = ones
    held[23:24, :] = norms[0]
    held[24:28, :] = low
    held[28:29, :] = norms[1]
    held[29:30, :] = norms[2]
    held[30:32, :] = jnp.zeros((2, points.shape[1]), F32)


def near_norms(points, weights, drift):
    shifted = drift * points
    return (-0.5 * square_sum(shifted), -0.5 * square_sum(points) + jnp.log(weights))


def first_kernel(
    deep, gathered_ref, points_hbm, weights_hbm, drift_hbm, sent_ref, sums_ref,
    held, near, far, scaled, sems, points_ref, weights_ref, drift_ref,
):
    arrivals = fetch((points_hbm, weights_hbm, drift_hbm), (points_ref, weights_ref, drift_ref), sems)
    chunks = gathered_ref.shape[0]
    for half in range(2):
        for chunk in range(chunks):
            columns = slice(chunk * LANES, (chunk + 1) * LANES)
            block = gathered_ref[chunk, HALF * half : HALF * (half + 1), :].astype(F32)
            pays, packed = block[:PAY], block[PAY:]
            far[half, columns, :] = far_factor(packed).T.astype(BF)
            for factor in range(FACTORS):
                scaled[half, PAY * factor : PAY * (factor + 1), columns] = (
                    pays * packed[factor : factor + 1]
                ).astype(BF)
            scaled[half, PAY * FACTORS :, columns] = pays.astype(BF)
    arrive(arrivals)
    points = points_ref[...]
    drift = row_of(drift_ref, points)
    norms = near_norms(points, weights_ref[...], drift)
    for half in range(2):
        near_factor(points, norms[half], drift, held)
        near[half] = held[...].astype(BF)
    for half in range(2):
        right = near[half]
        for start in range(0, chunks * LANES, deep):
            rows = slice(start, start + deep)
            power = jnp.dot(far[half, rows, :], right, preferred_element_type=F32)
            trans = jnp.exp(power).astype(BF)
            part = jnp.dot(scaled[half, :, rows], trans, preferred_element_type=F32)
            sums_ref[half] = part if start == 0 else sums_ref[half] + part
        last = sums_ref[half, PAY * FACTORS :, :].astype(BF)
        for chunk in range(sent_ref.shape[0]):
            sent_ref[chunk, PAY * half : PAY * (half + 1), :] = last[
                :, chunk * LANES : (chunk + 1) * LANES
            ]


def middle_kernel(index_ref, got_ref, exercise_hbm, payoff_hbm, after_hbm, out_ref, sems, exercise_ref, payoff_ref):
    columns = pl.ds(pl.multiple_of(index_ref[0] * LANES, LANES), LANES)
    arrivals = fetch(
        (exercise_hbm.at[:, columns], payoff_hbm.at[:, columns]), (exercise_ref, payoff_ref), sems
    )
    total = got_ref[0].astype(F32)
    for device in range(1, got_ref.shape[0]):
        total = total + got_ref[device].astype(F32)
    arrive(arrivals)
    mask = exercise_ref[...].astype(F32)
    values = mask * payoff_ref[...] + (1.0 - mask) * total[:PAY]
    cots = (1.0 - mask) * total[PAY:]
    packed = jnp.concatenate([values, cots], axis=0).astype(BF)
    for device in range(out_ref.shape[0]):
        out_ref[device] = packed


def weighted(pays, sums):
    return [
        jnp.sum(pays * sums[PAY * side : PAY * (side + 1)], axis=0, keepdims=True)
        for side in range(SIDES)
    ]


def own_kernel(middle_ref, points_hbm, drift_hbm, sums_ref, own_ref, sems, points_ref, drift_ref):
    arrive(fetch((points_hbm, drift_hbm), (points_ref, drift_ref), sems))
    for chunk in range(middle_ref.shape[0]):
        columns = slice(chunk * LANES, (chunk + 1) * LANES)
        after = weighted(middle_ref[chunk, PAY:, :].astype(F32), sums_ref[0, :, columns])
        before = weighted(middle_ref[chunk, :PAY, :].astype(F32), sums_ref[1, :, columns])
        for factor in range(FACTORS):
            rate = drift_ref[factor]
            place = points_ref[factor : factor + 1, columns]
            own_ref[chunk, factor : factor + 1, :] = rate * (
                after[factor] - rate * place * after[FACTORS]
            ) - (place * before[FACTORS] - rate * before[factor])


def ahead_kernel(
    half, first, deep, gathered_ref, points_hbm, weights_hbm, drift_hbm, after_hbm, trans_hbm,
    held, near, far, kept, sems, points_ref, weights_ref, drift_ref, more,
):
    arrivals = fetch((points_hbm, weights_hbm, drift_hbm), (points_ref, weights_ref, drift_ref), sems)
    for chunk in range(gathered_ref.shape[0]):
        far[:, chunk * LANES : (chunk + 1) * LANES] = far_factor(
            gathered_ref[chunk, HALF * half + PAY : HALF * (half + 1), :].astype(F32)
        ).astype(BF)
    arrive(arrivals)
    count = kept.shape[0]
    points = points_ref[:, first : first + count]
    drift = row_of(drift_ref, points)
    near_factor(points, near_norms(points, weights_ref[:, first : first + count], drift)[half], drift, held)
    near[...] = held[...].T.astype(BF)
    right = far[...]
    copies = []
    for start in range(0, count, deep):
        rows = slice(start, start + deep)
        power = jnp.dot(near[rows, :], right, preferred_element_type=F32)
        kept[rows, :] = jnp.exp(power).astype(BF)
        if (start + deep) % PIECE == 0:
            span = slice(start + deep - PIECE, start + deep)
            copies += fetch((kept.at[span],), (trans_hbm.at[span],), more.at[slice(len(copies), len(copies) + 1)])
    arrive(copies)


def second_kernel(
    deep, middle_ref, gathered_ref, points_hbm, weights_hbm, drift_hbm, end_hbm, root_hbm, sent_ref,
    held, total, near, far, scaled, kept, sems, more, points_ref, weights_ref, drift_ref,
):
    arrivals = fetch((points_hbm, weights_hbm, drift_hbm), (points_ref, weights_ref, drift_ref), sems)
    size = points_ref.shape[1]
    early = end_hbm.shape[0]
    blocks = [(0, start) for start in range(0, early, BLOCK)] + [(1, start) for start in range(0, size, BLOCK)]
    copies = [
        pltpu.make_async_copy(
            (end_hbm, root_hbm)[half].at[start : start + BLOCK, :],
            kept.at[BLOCK * number : BLOCK * (number + 1), :],
            more.at[number],
        )
        for number, (half, start) in enumerate(blocks)
    ]
    for copy in copies[:AHEAD]:
        copy.start()
    chunks = middle_ref.shape[0]
    for chunk in range(chunks):
        columns = slice(chunk * LANES, (chunk + 1) * LANES)
        far[:, columns] = far_factor(gathered_ref[chunk, PAY:HALF, :].astype(F32)).astype(BF)
    arrive(arrivals)
    points = points_ref[...]
    rounded = points.astype(BF).astype(F32)
    late = points[:, early:]
    drift = row_of(drift_ref, late)
    near_factor(late, near_norms(late, weights_ref[:, early:], drift)[0], drift, held)
    near[...] = held[...].T.astype(BF)
    for half in range(2):
        rows = slice(PAY * (1 - half), PAY * (2 - half))
        for chunk in range(chunks):
            columns = slice(chunk * LANES, (chunk + 1) * LANES)
            pays = middle_ref[chunk, rows, :].astype(F32)
            for factor in range(FACTORS):
                scaled[half, PAY * factor : PAY * (factor + 1), columns] = (
                    pays * rounded[factor : factor + 1, columns]
                ).astype(BF)
            scaled[half, PAY * FACTORS :, columns] = pays.astype(BF)
    right = far[...]
    for start in range(early, size, deep):
        power = jnp.dot(near[start - early : start - early + deep, :], right, preferred_element_type=F32)
        trans = jnp.exp(power).astype(BF)
        part = jnp.dot(scaled[0, :, start : start + deep], trans, preferred_element_type=F32)
        total[0] = part if start == early else total[0] + part
    for number, (half, start) in enumerate(blocks):
        copies[number].wait()
        for copy in copies[number + AHEAD : number + AHEAD + 1]:
            copy.start()
        part = jnp.dot(
            scaled[half, :, start : start + BLOCK],
            kept[BLOCK * number : BLOCK * (number + 1), :],
            preferred_element_type=F32,
        )
        total[half] = part if half == 1 and start == 0 else total[half] + part
    for chunk in range(chunks):
        columns = slice(chunk * LANES, (chunk + 1) * LANES)
        grads = []
        for half in range(2):
            part = total[half, :, columns]
            block = gathered_ref[chunk, HALF * half : HALF * (half + 1), :].astype(F32)
            sides = weighted(block[:PAY], part)
            place = block[PAY : PAY + 4] + block[PAY + 4 : PAY + 8] + block[PAY + 8 : PAY + 12]
            for factor in range(FACTORS):
                rate = drift_ref[factor]
                spot = place[factor : factor + 1]
                if half == 0:
                    grads.append(rate * sides[factor] - spot * sides[FACTORS])
                else:
                    grads.append(rate * (sides[factor] - rate * spot * sides[FACTORS]))
        for row, grad in enumerate(grads):
            held[row : row + 1, 0:LANES] = grad
        held[8:16, 0:LANES] = jnp.zeros((8, LANES), F32)
        sent_ref[chunk, 0:PAY, :] = total[0, PAY * FACTORS :, columns].astype(BF)
        sent_ref[chunk, PAY:, :] = held[0:16, 0:LANES].astype(BF)


def last_kernel(got_ref, own_ref, terminal_ref, root_ref, mid_ref, end_ref):
    total = got_ref[0].astype(F32)
    own = own_ref[0]
    for device in range(1, got_ref.shape[0]):
        total = total + got_ref[device].astype(F32)
        own = own + own_ref[device]
    terminal_ref[...] = total[:PAY]
    end_ref[...] = total[PAY : PAY + FACTORS]
    root_ref[...] = total[PAY + FACTORS : PAY + 2 * FACTORS]
    mid_ref[...] = own


VMEM = pl.BlockSpec(memory_space=pltpu.VMEM)
HBM = pl.BlockSpec(memory_space=pltpu.HBM)
ANY = pl.BlockSpec(memory_space=pl.ANY)
SMEM = pl.BlockSpec(memory_space=pltpu.SMEM)
PARAMS = pltpu.CompilerParams(vmem_limit_bytes=LIMIT)


def shape(dims, dtype):
    return jax.ShapeDtypeStruct(dims, dtype)


def held_back(*arrays):
    return [pltpu.with_memory_space_constraint(array, pltpu.HBM) for array in arrays]


def staged(*arrays):
    blocks = [pltpu.VMEM(array.shape, array.dtype) for array in arrays[:-1]]
    return blocks + [pltpu.SMEM(arrays[-1].shape, arrays[-1].dtype)]


def pack_call(count, *arrays):
    return pl.pallas_call(
        pack_kernel,
        out_shape=shape((count, 2 * HALF, LANES), BF),
        in_specs=[HBM] * 7,
        out_specs=VMEM,
        scratch_shapes=[pltpu.VMEM((2 * HALF, LANES), F32), pltpu.SemaphoreType.DMA((7,))]
        + staged(*arrays),
        compiler_params=PARAMS,
    )(*held_back(*arrays))


def first_call(gathered, points, weights, drift):
    count, size = gathered.shape[0], points.shape[1]
    deep = DEEP
    return pl.pallas_call(
        functools.partial(first_kernel, deep),
        out_shape=(
            shape((size // LANES, 2 * PAY, LANES), BF),
            shape((2, SIDES * PAY, size), F32),
        ),
        in_specs=[VMEM] + [HBM] * 3,
        out_specs=(VMEM, VMEM),
        scratch_shapes=[
            pltpu.VMEM((DEPTH, size), F32),
            pltpu.VMEM((2, DEPTH, size), BF),
            pltpu.VMEM((2, count * LANES, DEPTH), BF),
            pltpu.VMEM((2, SIDES * PAY, count * LANES), BF),
            pltpu.SemaphoreType.DMA((3,)),
        ]
        + staged(points, weights, drift),
        compiler_params=PARAMS,
    )(gathered, *held_back(points, weights, drift))


def middle_call(index, got, exercise, payoff, after):
    return pl.pallas_call(
        middle_kernel,
        out_shape=shape(got.shape, BF),
        in_specs=[SMEM, VMEM, HBM, HBM, HBM],
        out_specs=VMEM,
        scratch_shapes=[
            pltpu.SemaphoreType.DMA((2,)),
            pltpu.VMEM((PAY, LANES), jnp.int32),
            pltpu.VMEM((PAY, LANES), F32),
        ],
        compiler_params=PARAMS,
    )(index, got, *held_back(exercise, payoff, after))


def own_call(middle, points, drift, sums):
    return pl.pallas_call(
        own_kernel,
        out_shape=shape((middle.shape[0], FACTORS, LANES), F32),
        in_specs=[VMEM, HBM, HBM, VMEM],
        out_specs=VMEM,
        scratch_shapes=[pltpu.SemaphoreType.DMA((2,))] + staged(points, drift),
        compiler_params=PARAMS,
    )(middle, *held_back(points, drift), sums)


def ahead_call(half, first, count, gathered, points, weights, drift, after):
    size = points.shape[1]
    width = gathered.shape[0] * LANES
    return pl.pallas_call(
        functools.partial(ahead_kernel, half, first, DEEP),
        out_shape=pltpu.HBM((count, width), BF),
        in_specs=[VMEM] + [HBM] * 3 + [ANY],
        out_specs=HBM,
        scratch_shapes=[
            pltpu.VMEM((DEPTH, count), F32),
            pltpu.VMEM((count, DEPTH), BF),
            pltpu.VMEM((DEPTH, width), BF),
            pltpu.VMEM((count, width), BF),
            pltpu.SemaphoreType.DMA((3,)),
        ]
        + staged(points, weights, drift)
        + [pltpu.SemaphoreType.DMA((count // PIECE,))],
        compiler_params=PARAMS,
        cost_estimate=pl.CostEstimate(
            flops=2 * 256 * count * width, bytes_accessed=2 * count * width, transcendentals=count * width
        ),
    )(gathered, *held_back(points, weights, drift), after)


def second_call(middle, gathered, points, weights, drift, end_trans, root_trans):
    count, size = gathered.shape[0], points.shape[1]
    width = count * LANES
    early = end_trans.shape[0]
    blocks = (early + size) // BLOCK
    return pl.pallas_call(
        functools.partial(second_kernel, DEEP),
        out_shape=shape((count, HALF, LANES), BF),
        in_specs=[VMEM] * 2 + [HBM] * 5,
        out_specs=VMEM,
        scratch_shapes=[
            pltpu.VMEM((DEPTH, size - early), F32),
            pltpu.VMEM((2, SIDES * PAY, width), F32),
            pltpu.VMEM((size - early, DEPTH), BF),
            pltpu.VMEM((DEPTH, width), BF),
            pltpu.VMEM((2, SIDES * PAY, size), BF),
            pltpu.VMEM((early + size, width), BF),
            pltpu.SemaphoreType.DMA((3,)),
            pltpu.SemaphoreType.DMA((blocks,)),
        ]
        + staged(points, weights, drift),
        compiler_params=PARAMS,
        cost_estimate=pl.CostEstimate(
            flops=4 * SIDES * PAY * size * size, bytes_accessed=4 * size * size, transcendentals=size * size
        ),
    )(middle, gathered, *held_back(points, weights, drift, end_trans, root_trans))


def last_call(got, own):
    return pl.pallas_call(
        last_kernel,
        out_shape=(shape((PAY, LANES), F32),) + (shape((FACTORS, LANES), F32),) * 3,
        in_specs=[VMEM] * 2,
        out_specs=(VMEM,) * 4,
        compiler_params=PARAMS,
    )(got, own)


def exchange(blocks, axis):
    return lax.all_to_all(blocks, axis, 0, 0)


def on_device(
    root_cot,
    root_exercise,
    mid_exercise,
    mid_payoff,
    end_values,
    root_points,
    mid_points,
    end_points,
    mid_weights,
    end_weights,
    drift_rate,
):
    rows = lax.axis_size("row")
    weights = mid_weights[None, :]
    packed = pack_call(
        rows, root_cot, root_exercise, end_values, root_points, end_points, end_weights[None, :], drift_rate
    )
    gathered = exchange(packed, "row")
    parts, sums = first_call(gathered, mid_points, weights, drift_rate)
    got = exchange(parts, "col")
    root_trans = ahead_call(1, 0, mid_points.shape[1], gathered, mid_points, weights, drift_rate, parts)
    values = middle_call(lax.axis_index("col")[None], got, mid_exercise, mid_payoff, root_trans)
    middle = exchange(values, "col")
    end_trans = ahead_call(0, 0, EARLY, gathered, mid_points, weights, drift_rate, values)
    own = exchange(own_call(middle, mid_points, drift_rate, sums), "col")
    sides = second_call(middle, gathered, mid_points, weights, drift_rate, end_trans, root_trans)
    far = exchange(sides, "row")
    terminal, grad_root, grad_mid, grad_end = last_call(far, own)
    return (terminal, grad_root, grad_mid, grad_end)


def solution(mesh):
    in_specs = (
        P(None, ("col", "row")),
        P(None, ("col", "row")),
        P(None, "row"),
        P(None, "row"),
        P(None, ("col", "row")),
        P(None, ("col", "row")),
        P(None, "row"),
        P(None, ("col", "row")),
        P("row"),
        P(("col", "row")),
        P(),
    )
    out_specs = (
        P(None, ("col", "row")),
        P(None, ("col", "row")),
        P(None, ("row", "col")),
        P(None, ("col", "row")),
    )
    return jax.shard_map(
        on_device, mesh=mesh, in_specs=in_specs, out_specs=out_specs, check_vma=False
    )
```

```python
import functools

import jax
import jax.numpy as jnp
from jax import lax
from jax.experimental import pallas as pl
from jax.experimental.pallas import tpu as pltpu
from jax.sharding import PartitionSpec as P

BF = jnp.bfloat16
F32 = jnp.float32
LANES = 128
PAY = 32
FACTORS = 4
SIDES = FACTORS + 1
HALF = 48
DEPTH = 32
DEEP = 256
PIECE = 512
BLOCK = 1024
AHEAD = 2
EARLY = 1024
LIMIT = 36 * 1024 * 1024


def split3(value):
    high = value.astype(BF).astype(F32)
    rest = value - high
    middle = rest.astype(BF).astype(F32)
    return high, middle, (rest - middle).astype(BF).astype(F32)


def row_of(drift_ref, points):
    rows = lax.broadcasted_iota(jnp.int32, points.shape, 0)
    out = jnp.zeros(points.shape, F32)
    for factor in range(FACTORS):
        out = jnp.where(rows == factor, drift_ref[factor], out)
    return out


def square_sum(points):
    return jnp.sum(points * points, axis=0, keepdims=True)


def fetch(sources, places, sems):
    copies = [
        pltpu.make_async_copy(source, place, sems.at[number])
        for number, (source, place) in enumerate(zip(sources, places))
    ]
    for copy in copies:
        copy.start()
    return copies


def arrive(copies):
    for copy in copies:
        copy.wait()


def pack_kernel(
    cot_hbm, exercise_hbm, values_hbm, root_hbm, end_hbm, weight_hbm, drift_hbm, out_ref,
    held, sems, cot_ref, exercise_ref, values_ref, root_ref, end_ref, weight_ref, drift_ref,
):
    arrive(
        fetch(
            (cot_hbm, exercise_hbm, values_hbm, root_hbm, end_hbm, weight_hbm, drift_hbm),
            (cot_ref, exercise_ref, values_ref, root_ref, end_ref, weight_ref, drift_ref),
            sems,
        )
    )
    mask = 1.0 - exercise_ref[...].astype(F32)
    root = root_ref[...]
    end = end_ref[...]
    shifted = row_of(drift_ref, root) * root
    norms = (-0.5 * square_sum(end) + jnp.log(weight_ref[...]), -0.5 * square_sum(shifted))
    values = (values_ref[...].astype(F32), cot_ref[...].astype(F32) * mask)
    for half, (points, norm, pays) in enumerate(zip((end, root), norms, values)):
        base = HALF * half
        held[base : base + PAY, :] = pays
        for part, piece in enumerate(split3(points)):
            start = base + PAY + FACTORS * part
            held[start : start + FACTORS, :] = piece
        for part, piece in enumerate(split3(norm)):
            start = base + PAY + 3 * FACTORS + part
            held[start : start + 1, :] = piece
        held[base + HALF - 1 : base + HALF, :] = jnp.ones((1, LANES), F32)
    packed = held[...].astype(BF)
    for device in range(out_ref.shape[0]):
        out_ref[device] = packed


def far_factor(block):
    rows = lax.broadcasted_iota(jnp.int32, (8, block.shape[1]), 0)
    last = jnp.where(rows < FACTORS, block[0:8], jnp.where(rows < FACTORS + 2, 1.0, 0.0))
    return jnp.concatenate([block[0:8], block[0:8], block[8:16], last], axis=0)


def near_factor(points, norm, drift, held):
    high, middle, low = split3(drift * points)
    norms = split3(norm)
    ones = jnp.ones((3, points.shape[1]), F32)
    held[0:4, :] = high
    held[4:8, :] = high
    held[8:12, :] = middle
    held[12:16, :] = middle
    held[16:20, :] = high
    held[20:23, :] = ones
    held[23:24, :] = norms[0]
    held[24:28, :] = low
    held[28:29, :] = norms[1]
    held[29:30, :] = norms[2]
    held[30:32, :] = jnp.zeros((2, points.shape[1]), F32)


def near_norms(points, weights, drift):
    shifted = drift * points
    return (-0.5 * square_sum(shifted), -0.5 * square_sum(points) + jnp.log(weights))


def near_kernel(points_hbm, weights_hbm, drift_hbm, near_ref, held, sems, points_ref, weights_ref, drift_ref):
    arrive(fetch((points_hbm, weights_hbm, drift_hbm), (points_ref, weights_ref, drift_ref), sems))
    points = points_ref[...]
    drift = row_of(drift_ref, points)
    norms = near_norms(points, weights_ref[...], drift)
    for half in range(2):
        near_factor(points, norms[half], drift, held)
        near_ref[half] = held[...].astype(BF)


def first_kernel(deep, gathered_ref, near, sent_ref, sums_ref, far, scaled):
    chunks = gathered_ref.shape[0]
    for half in range(2):
        for chunk in range(chunks):
            columns = slice(chunk * LANES, (chunk + 1) * LANES)
            block = gathered_ref[chunk, HALF * half : HALF * (half + 1), :].astype(F32)
            pays, packed = block[:PAY], block[PAY:]
            far[half, columns, :] = far_factor(packed).T.astype(BF)
            for factor in range(FACTORS):
                scaled[half, PAY * factor : PAY * (factor + 1), columns] = (
                    pays * packed[factor : factor + 1]
                ).astype(BF)
            scaled[half, PAY * FACTORS :, columns] = pays.astype(BF)
    for half in range(2):
        right = near[half]
        for start in range(0, chunks * LANES, deep):
            rows = slice(start, start + deep)
            power = jnp.dot(far[half, rows, :], right, preferred_element_type=F32)
            trans = jnp.exp(power).astype(BF)
            part = jnp.dot(scaled[half, :, rows], trans, preferred_element_type=F32)
            sums_ref[half] = part if start == 0 else sums_ref[half] + part
        last = sums_ref[half, PAY * FACTORS :, :].astype(BF)
        for chunk in range(sent_ref.shape[0]):
            sent_ref[chunk, PAY * half : PAY * (half + 1), :] = last[
                :, chunk * LANES : (chunk + 1) * LANES
            ]


def middle_kernel(index_ref, got_ref, exercise_hbm, payoff_hbm, after_hbm, out_ref, mark_ref, sems, exercise_ref, payoff_ref):
    columns = pl.ds(pl.multiple_of(index_ref[0] * LANES, LANES), LANES)
    arrivals = fetch(
        (exercise_hbm.at[:, columns], payoff_hbm.at[:, columns]), (exercise_ref, payoff_ref), sems
    )
    total = got_ref[0].astype(F32)
    for device in range(1, got_ref.shape[0]):
        total = total + got_ref[device].astype(F32)
    arrive(arrivals)
    mask = exercise_ref[...].astype(F32)
    values = mask * payoff_ref[...] + (1.0 - mask) * total[:PAY]
    cots = (1.0 - mask) * total[PAY:]
    packed = jnp.concatenate([values, cots], axis=0).astype(BF)
    for device in range(out_ref.shape[0]):
        out_ref[device] = packed
    mark_ref[...] = values[0:8]


def weighted(pays, sums):
    return [
        jnp.sum(pays * sums[PAY * side : PAY * (side + 1)], axis=0, keepdims=True)
        for side in range(SIDES)
    ]


def own_kernel(middle_ref, points_hbm, drift_hbm, sums_ref, own_ref, sems, points_ref, drift_ref):
    arrive(fetch((points_hbm, drift_hbm), (points_ref, drift_ref), sems))
    for chunk in range(middle_ref.shape[0]):
        columns = slice(chunk * LANES, (chunk + 1) * LANES)
        after = weighted(middle_ref[chunk, PAY:, :].astype(F32), sums_ref[0, :, columns])
        before = weighted(middle_ref[chunk, :PAY, :].astype(F32), sums_ref[1, :, columns])
        for factor in range(FACTORS):
            rate = drift_ref[factor]
            place = points_ref[factor : factor + 1, columns]
            own_ref[chunk, factor : factor + 1, :] = rate * (
                after[factor] - rate * place * after[FACTORS]
            ) - (place * before[FACTORS] - rate * before[factor])


def ahead_kernel(
    half, first, deep, gathered_ref, points_hbm, weights_hbm, drift_hbm, after_hbm, trans_hbm,
    held, near, far, kept, sems, points_ref, weights_ref, drift_ref, more,
):
    arrivals = fetch((points_hbm, weights_hbm, drift_hbm), (points_ref, weights_ref, drift_ref), sems)
    for chunk in range(gathered_ref.shape[0]):
        far[:, chunk * LANES : (chunk + 1) * LANES] = far_factor(
            gathered_ref[chunk, HALF * half + PAY : HALF * (half + 1), :].astype(F32)
        ).astype(BF)
    arrive(arrivals)
    count = kept.shape[0]
    points = points_ref[:, first : first + count]
    drift = row_of(drift_ref, points)
    near_factor(points, near_norms(points, weights_ref[:, first : first + count], drift)[half], drift, held)
    near[...] = held[...].T.astype(BF)
    right = far[...]
    copies = []
    for start in range(0, count, deep):
        rows = slice(start, start + deep)
        power = jnp.dot(near[rows, :], right, preferred_element_type=F32)
        kept[rows, :] = jnp.exp(power).astype(BF)
        if (start + deep) % PIECE == 0:
            span = slice(start + deep - PIECE, start + deep)
            copies += fetch((kept.at[span],), (trans_hbm.at[span],), more.at[slice(len(copies), len(copies) + 1)])
    arrive(copies)


def second_kernel(
    deep, middle_ref, gathered_ref, points_hbm, weights_hbm, drift_hbm, end_hbm, root_hbm, sent_ref,
    held, total, near, far, scaled, kept, sems, more, points_ref, weights_ref, drift_ref,
):
    arrivals = fetch((points_hbm, weights_hbm, drift_hbm), (points_ref, weights_ref, drift_ref), sems)
    size = points_ref.shape[1]
    early = end_hbm.shape[0]
    blocks = [(0, start) for start in range(0, early, BLOCK)] + [(1, start) for start in range(0, size, BLOCK)]
    copies = [
        pltpu.make_async_copy(
            (end_hbm, root_hbm)[half].at[start : start + BLOCK, :],
            kept.at[BLOCK * number : BLOCK * (number + 1), :],
            more.at[number],
        )
        for number, (half, start) in enumerate(blocks)
    ]
    for copy in copies[:AHEAD]:
        copy.start()
    chunks = middle_ref.shape[0]
    for chunk in range(chunks):
        columns = slice(chunk * LANES, (chunk + 1) * LANES)
        far[:, columns] = far_factor(gathered_ref[chunk, PAY:HALF, :].astype(F32)).astype(BF)
    arrive(arrivals)
    points = points_ref[...]
    rounded = points.astype(BF).astype(F32)
    late = points[:, early:]
    drift = row_of(drift_ref, late)
    near_factor(late, near_norms(late, weights_ref[:, early:], drift)[0], drift, held)
    near[...] = held[...].T.astype(BF)
    for half in range(2):
        rows = slice(PAY * (1 - half), PAY * (2 - half))
        for chunk in range(chunks):
            columns = slice(chunk * LANES, (chunk + 1) * LANES)
            pays = middle_ref[chunk, rows, :].astype(F32)
            for factor in range(FACTORS):
                scaled[half, PAY * factor : PAY * (factor + 1), columns] = (
                    pays * rounded[factor : factor + 1, columns]
                ).astype(BF)
            scaled[half, PAY * FACTORS :, columns] = pays.astype(BF)
    right = far[...]
    for start in range(early, size, deep):
        power = jnp.dot(near[start - early : start - early + deep, :], right, preferred_element_type=F32)
        trans = jnp.exp(power).astype(BF)
        part = jnp.dot(scaled[0, :, start : start + deep], trans, preferred_element_type=F32)
        total[0] = part if start == early else total[0] + part
    for number, (half, start) in enumerate(blocks):
        copies[number].wait()
        for copy in copies[number + AHEAD : number + AHEAD + 1]:
            copy.start()
        part = jnp.dot(
            scaled[half, :, start : start + BLOCK],
            kept[BLOCK * number : BLOCK * (number + 1), :],
            preferred_element_type=F32,
        )
        total[half] = part if half == 1 and start == 0 else total[half] + part
    for chunk in range(chunks):
        columns = slice(chunk * LANES, (chunk + 1) * LANES)
        grads = []
        for half in range(2):
            part = total[half, :, columns]
            block = gathered_ref[chunk, HALF * half : HALF * (half + 1), :].astype(F32)
            sides = weighted(block[:PAY], part)
            place = block[PAY : PAY + 4] + block[PAY + 4 : PAY + 8] + block[PAY + 8 : PAY + 12]
            for factor in range(FACTORS):
                rate = drift_ref[factor]
                spot = place[factor : factor + 1]
                if half == 0:
                    grads.append(rate * sides[factor] - spot * sides[FACTORS])
                else:
                    grads.append(rate * (sides[factor] - rate * spot * sides[FACTORS]))
        for row, grad in enumerate(grads):
            held[row : row + 1, 0:LANES] = grad
        sent_ref[chunk] = jnp.concatenate(
            [total[0, PAY * FACTORS :, columns], held[0 : 2 * FACTORS, 0:LANES]], axis=0
        ).astype(BF)


def last_kernel(got_ref, own_ref, terminal_ref, root_ref, mid_ref, end_ref):
    total = got_ref[0].astype(F32)
    own = own_ref[0]
    for device in range(1, got_ref.shape[0]):
        total = total + got_ref[device].astype(F32)
        own = own + own_ref[device]
    terminal_ref[...] = total[:PAY]
    end_ref[...] = total[PAY : PAY + FACTORS]
    root_ref[...] = total[PAY + FACTORS : PAY + 2 * FACTORS]
    mid_ref[...] = own


VMEM = pl.BlockSpec(memory_space=pltpu.VMEM)
HBM = pl.BlockSpec(memory_space=pltpu.HBM)
ANY = pl.BlockSpec(memory_space=pl.ANY)
SMEM = pl.BlockSpec(memory_space=pltpu.SMEM)
PARAMS = pltpu.CompilerParams(vmem_limit_bytes=LIMIT)


def shape(dims, dtype):
    return jax.ShapeDtypeStruct(dims, dtype)


def held_back(*arrays):
    return [pltpu.with_memory_space_constraint(array, pltpu.HBM) for array in arrays]


def staged(*arrays):
    blocks = [pltpu.VMEM(array.shape, array.dtype) for array in arrays[:-1]]
    return blocks + [pltpu.SMEM(arrays[-1].shape, arrays[-1].dtype)]


def pack_call(count, *arrays):
    return pl.pallas_call(
        pack_kernel,
        out_shape=shape((count, 2 * HALF, LANES), BF),
        in_specs=[HBM] * 7,
        out_specs=VMEM,
        scratch_shapes=[pltpu.VMEM((2 * HALF, LANES), F32), pltpu.SemaphoreType.DMA((7,))]
        + staged(*arrays),
        compiler_params=PARAMS,
    )(*held_back(*arrays))


def near_call(points, weights, drift):
    size = points.shape[1]
    return pl.pallas_call(
        near_kernel,
        out_shape=shape((2, DEPTH, size), BF),
        in_specs=[HBM] * 3,
        out_specs=VMEM,
        scratch_shapes=[pltpu.VMEM((DEPTH, size), F32), pltpu.SemaphoreType.DMA((3,))]
        + staged(points, weights, drift),
        compiler_params=PARAMS,
    )(*held_back(points, weights, drift))


def first_call(gathered, near):
    count, size = gathered.shape[0], near.shape[2]
    return pl.pallas_call(
        functools.partial(first_kernel, DEEP),
        out_shape=(
            shape((size // LANES, 2 * PAY, LANES), BF),
            pltpu.VMEM((2, SIDES * PAY, size), F32),
        ),
        in_specs=[VMEM] * 2,
        out_specs=(VMEM, VMEM),
        scratch_shapes=[
            pltpu.VMEM((2, count * LANES, DEPTH), BF),
            pltpu.VMEM((2, SIDES * PAY, count * LANES), BF),
        ],
        compiler_params=PARAMS,
    )(gathered, near)


def middle_call(index, got, exercise, payoff, after):
    return pl.pallas_call(
        middle_kernel,
        out_shape=(shape(got.shape, BF), shape((8, LANES), F32)),
        in_specs=[SMEM, VMEM, HBM, HBM, HBM],
        out_specs=(VMEM, VMEM),
        scratch_shapes=[
            pltpu.SemaphoreType.DMA((2,)),
            pltpu.VMEM((PAY, LANES), jnp.int32),
            pltpu.VMEM((PAY, LANES), F32),
        ],
        compiler_params=PARAMS,
    )(index, got, *held_back(exercise, payoff, after))


def own_call(middle, points, drift, sums):
    return pl.pallas_call(
        own_kernel,
        out_shape=shape((middle.shape[0], FACTORS, LANES), F32),
        in_specs=[VMEM, HBM, HBM, VMEM],
        out_specs=VMEM,
        scratch_shapes=[pltpu.SemaphoreType.DMA((2,))] + staged(points, drift),
        compiler_params=PARAMS,
    )(middle, *held_back(points, drift), sums)


def ahead_call(half, first, count, gathered, points, weights, drift, after):
    size = points.shape[1]
    width = gathered.shape[0] * LANES
    return pl.pallas_call(
        functools.partial(ahead_kernel, half, first, DEEP),
        out_shape=pltpu.HBM((count, width), BF),
        in_specs=[VMEM] + [HBM] * 3 + [ANY],
        out_specs=HBM,
        scratch_shapes=[
            pltpu.VMEM((DEPTH, count), F32),
            pltpu.VMEM((count, DEPTH), BF),
            pltpu.VMEM((DEPTH, width), BF),
            pltpu.VMEM((count, width), BF),
            pltpu.SemaphoreType.DMA((3,)),
        ]
        + staged(points, weights, drift)
        + [pltpu.SemaphoreType.DMA((count // PIECE,))],
        compiler_params=PARAMS,
        cost_estimate=pl.CostEstimate(
            flops=2 * 256 * count * width, bytes_accessed=2 * count * width, transcendentals=count * width
        ),
    )(gathered, *held_back(points, weights, drift), after)


def second_call(middle, gathered, points, weights, drift, end_trans, root_trans):
    count, size = gathered.shape[0], points.shape[1]
    width = count * LANES
    early = end_trans.shape[0]
    blocks = (early + size) // BLOCK
    return pl.pallas_call(
        functools.partial(second_kernel, DEEP),
        out_shape=shape((count, PAY + 2 * FACTORS, LANES), BF),
        in_specs=[VMEM] * 2 + [HBM] * 5,
        out_specs=VMEM,
        scratch_shapes=[
            pltpu.VMEM((DEPTH, size - early), F32),
            pltpu.VMEM((2, SIDES * PAY, width), F32),
            pltpu.VMEM((size - early, DEPTH), BF),
            pltpu.VMEM((DEPTH, width), BF),
            pltpu.VMEM((2, SIDES * PAY, size), BF),
            pltpu.VMEM((early + size, width), BF),
            pltpu.SemaphoreType.DMA((3,)),
            pltpu.SemaphoreType.DMA((blocks,)),
        ]
        + staged(points, weights, drift),
        compiler_params=PARAMS,
        cost_estimate=pl.CostEstimate(
            flops=4 * SIDES * PAY * size * size, bytes_accessed=4 * size * size, transcendentals=size * size
        ),
    )(middle, gathered, *held_back(points, weights, drift, end_trans, root_trans))


def last_call(got, own):
    return pl.pallas_call(
        last_kernel,
        out_shape=(shape((PAY, LANES), F32),) + (shape((FACTORS, LANES), F32),) * 3,
        in_specs=[VMEM] * 2,
        out_specs=(VMEM,) * 4,
        compiler_params=PARAMS,
    )(got, own)


def exchange(blocks, axis):
    return lax.all_to_all(blocks, axis, 0, 0)


def on_device(
    root_cot,
    root_exercise,
    mid_exercise,
    mid_payoff,
    end_values,
    root_points,
    mid_points,
    end_points,
    mid_weights,
    end_weights,
    drift_rate,
):
    rows = lax.axis_size("row")
    weights = mid_weights[None, :]
    packed = pack_call(
        rows, root_cot, root_exercise, end_values, root_points, end_points, end_weights[None, :], drift_rate
    )
    gathered = exchange(packed, "row")
    near = near_call(mid_points, weights, drift_rate)
    parts, sums = first_call(gathered, near)
    got = exchange(parts, "col")
    root_trans = ahead_call(1, 0, mid_points.shape[1], gathered, mid_points, weights, drift_rate, parts)
    values, mark = middle_call(lax.axis_index("col")[None], got, mid_exercise, mid_payoff, root_trans)
    middle = exchange(values, "col")
    end_trans = ahead_call(0, 0, EARLY, gathered, mid_points, weights, drift_rate, mark)
    own = exchange(own_call(middle, mid_points, drift_rate, sums), "col")
    sides = second_call(middle, gathered, mid_points, weights, drift_rate, end_trans, root_trans)
    far = exchange(sides, "row")
    terminal, grad_root, grad_mid, grad_end = last_call(far, own)
    return (terminal, grad_root, grad_mid, grad_end)


def solution(mesh):
    in_specs = (
        P(None, ("col", "row")),
        P(None, ("col", "row")),
        P(None, "row"),
        P(None, "row"),
        P(None, ("col", "row")),
        P(None, ("col", "row")),
        P(None, "row"),
        P(None, ("col", "row")),
        P("row"),
        P(("col", "row")),
        P(),
    )
    out_specs = (
        P(None, ("col", "row")),
        P(None, ("col", "row")),
        P(None, ("row", "col")),
        P(None, ("col", "row")),
    )
    return jax.shard_map(
        on_device, mesh=mesh, in_specs=in_specs, out_specs=out_specs, check_vma=False
    )
```

```python
import functools

import jax
import jax.numpy as jnp
from jax import lax
from jax.experimental import pallas as pl
from jax.experimental.pallas import tpu as pltpu
from jax.sharding import PartitionSpec as P

BF = jnp.bfloat16
F32 = jnp.float32
LANES = 128
PAY = 32
FACTORS = 4
SIDES = FACTORS + 1
HALF = 48
DEPTH = 32
DEEP = 256
PIECE = 512
BLOCK = 1024
AHEAD = 2
EARLY = 1024
LIMIT = 36 * 1024 * 1024


def split3(value):
    high = value.astype(BF).astype(F32)
    rest = value - high
    middle = rest.astype(BF).astype(F32)
    return high, middle, (rest - middle).astype(BF).astype(F32)


def row_of(drift_ref, points):
    rows = lax.broadcasted_iota(jnp.int32, points.shape, 0)
    out = jnp.zeros(points.shape, F32)
    for factor in range(FACTORS):
        out = jnp.where(rows == factor, drift_ref[factor], out)
    return out


def square_sum(points):
    return jnp.sum(points * points, axis=0, keepdims=True)


def fetch(sources, places, sems):
    copies = [
        pltpu.make_async_copy(source, place, sems.at[number])
        for number, (source, place) in enumerate(zip(sources, places))
    ]
    for copy in copies:
        copy.start()
    return copies


def arrive(copies):
    for copy in copies:
        copy.wait()


def pack_kernel(
    cot_hbm, exercise_hbm, values_hbm, root_hbm, end_hbm, weight_hbm, drift_hbm, out_ref,
    held, sems, cot_ref, exercise_ref, values_ref, root_ref, end_ref, weight_ref, drift_ref,
):
    arrive(
        fetch(
            (cot_hbm, exercise_hbm, values_hbm, root_hbm, end_hbm, weight_hbm, drift_hbm),
            (cot_ref, exercise_ref, values_ref, root_ref, end_ref, weight_ref, drift_ref),
            sems,
        )
    )
    mask = 1.0 - exercise_ref[...].astype(F32)
    root = root_ref[...]
    end = end_ref[...]
    shifted = row_of(drift_ref, root) * root
    norms = (-0.5 * square_sum(end) + jnp.log(weight_ref[...]), -0.5 * square_sum(shifted))
    values = (values_ref[...].astype(F32), cot_ref[...].astype(F32) * mask)
    for half, (points, norm, pays) in enumerate(zip((end, root), norms, values)):
        base = HALF * half
        held[base : base + PAY, :] = pays
        for part, piece in enumerate(split3(points)):
            start = base + PAY + FACTORS * part
            held[start : start + FACTORS, :] = piece
        for part, piece in enumerate(split3(norm)):
            start = base + PAY + 3 * FACTORS + part
            held[start : start + 1, :] = piece
        held[base + HALF - 1 : base + HALF, :] = jnp.ones((1, LANES), F32)
    packed = held[...].astype(BF)
    for device in range(out_ref.shape[0]):
        out_ref[device] = packed


def far_factor(block):
    rows = lax.broadcasted_iota(jnp.int32, (8, block.shape[1]), 0)
    last = jnp.where(rows < FACTORS, block[0:8], jnp.where(rows < FACTORS + 2, 1.0, 0.0))
    return jnp.concatenate([block[0:8], block[0:8], block[8:16], last], axis=0)


def near_factor(points, norm, drift, held):
    high, middle, low = split3(drift * points)
    norms = split3(norm)
    ones = jnp.ones((3, points.shape[1]), F32)
    held[0:4, :] = high
    held[4:8, :] = high
    held[8:12, :] = middle
    held[12:16, :] = middle
    held[16:20, :] = high
    held[20:23, :] = ones
    held[23:24, :] = norms[0]
    held[24:28, :] = low
    held[28:29, :] = norms[1]
    held[29:30, :] = norms[2]
    held[30:32, :] = jnp.zeros((2, points.shape[1]), F32)


def near_norms(points, weights, drift):
    shifted = drift * points
    return (-0.5 * square_sum(shifted), -0.5 * square_sum(points) + jnp.log(weights))


def near_kernel(points_hbm, weights_hbm, drift_hbm, near_ref, table_ref, held, sems, points_ref, weights_ref, drift_ref):
    arrive(fetch((points_hbm, weights_hbm, drift_hbm), (points_ref, weights_ref, drift_ref), sems))
    points = points_ref[...]
    drift = row_of(drift_ref, points)
    table_ref[0:FACTORS, :] = points
    table_ref[FACTORS:, :] = drift
    norms = near_norms(points, weights_ref[...], drift)
    for half in range(2):
        near_factor(points, norms[half], drift, held)
        near_ref[half] = held[...].astype(BF)


def first_kernel(deep, gathered_ref, near, table_ref, sent_ref, sums_ref, far, scaled):
    sums_ref[2 * SIDES * PAY :, :] = table_ref[...]
    chunks = gathered_ref.shape[0]
    for half in range(2):
        for chunk in range(chunks):
            columns = slice(chunk * LANES, (chunk + 1) * LANES)
            block = gathered_ref[chunk, HALF * half : HALF * (half + 1), :].astype(F32)
            pays, packed = block[:PAY], block[PAY:]
            far[half, columns, :] = far_factor(packed).T.astype(BF)
            for factor in range(FACTORS):
                scaled[half, PAY * factor : PAY * (factor + 1), columns] = (
                    pays * packed[factor : factor + 1]
                ).astype(BF)
            scaled[half, PAY * FACTORS :, columns] = pays.astype(BF)
    for half in range(2):
        right = near[half]
        for start in range(0, chunks * LANES, deep):
            rows = slice(start, start + deep)
            power = jnp.dot(far[half, rows, :], right, preferred_element_type=F32)
            trans = jnp.exp(power).astype(BF)
            part = jnp.dot(scaled[half, :, rows], trans, preferred_element_type=F32)
            place = slice(SIDES * PAY * half, SIDES * PAY * (half + 1))
            sums_ref[place, :] = part if start == 0 else sums_ref[place, :] + part
        last = sums_ref[SIDES * PAY * half + PAY * FACTORS : SIDES * PAY * (half + 1), :].astype(BF)
        for chunk in range(sent_ref.shape[0]):
            sent_ref[chunk, PAY * half : PAY * (half + 1), :] = last[
                :, chunk * LANES : (chunk + 1) * LANES
            ]


def middle_kernel(index_ref, got_ref, exercise_hbm, payoff_hbm, after_hbm, out_ref, mark_ref, sems, exercise_ref, payoff_ref):
    columns = pl.ds(pl.multiple_of(index_ref[0] * LANES, LANES), LANES)
    arrivals = fetch(
        (exercise_hbm.at[:, columns], payoff_hbm.at[:, columns]), (exercise_ref, payoff_ref), sems
    )
    total = got_ref[0].astype(F32)
    for device in range(1, got_ref.shape[0]):
        total = total + got_ref[device].astype(F32)
    arrive(arrivals)
    mask = exercise_ref[...].astype(F32)
    values = mask * payoff_ref[...] + (1.0 - mask) * total[:PAY]
    cots = (1.0 - mask) * total[PAY:]
    packed = jnp.concatenate([values, cots], axis=0).astype(BF)
    for device in range(out_ref.shape[0]):
        out_ref[device] = packed
    mark_ref[...] = values[0:8]


def weighted(pays, sums):
    return [
        jnp.sum(pays * sums[PAY * side : PAY * (side + 1)], axis=0, keepdims=True)
        for side in range(SIDES)
    ]


def own_kernel(middle_ref, sums_ref, own_ref):
    for chunk in range(middle_ref.shape[0]):
        columns = slice(chunk * LANES, (chunk + 1) * LANES)
        after = weighted(middle_ref[chunk, PAY:, :].astype(F32), sums_ref[: SIDES * PAY, columns])
        before = weighted(
            middle_ref[chunk, :PAY, :].astype(F32), sums_ref[SIDES * PAY : 2 * SIDES * PAY, columns]
        )
        for factor in range(FACTORS):
            row = 2 * SIDES * PAY + factor
            place = sums_ref[row : row + 1, columns]
            rate = sums_ref[row + FACTORS : row + FACTORS + 1, columns]
            own_ref[chunk, factor : factor + 1, :] = rate * (
                after[factor] - rate * place * after[FACTORS]
            ) - (place * before[FACTORS] - rate * before[factor])


def ahead_kernel(half, first, deep, gathered_ref, near_ref, after_hbm, trans_hbm, near, far, kept, more):
    for chunk in range(gathered_ref.shape[0]):
        far[:, chunk * LANES : (chunk + 1) * LANES] = far_factor(
            gathered_ref[chunk, HALF * half + PAY : HALF * (half + 1), :].astype(F32)
        ).astype(BF)
    count = kept.shape[0]
    near[...] = near_ref[half, :, first : first + count].astype(F32).T.astype(BF)
    right = far[...]
    copies = []
    for start in range(0, count, deep):
        rows = slice(start, start + deep)
        power = jnp.dot(near[rows, :], right, preferred_element_type=F32)
        kept[rows, :] = jnp.exp(power).astype(BF)
        if (start + deep) % PIECE == 0:
            span = slice(start + deep - PIECE, start + deep)
            copies += fetch((kept.at[span],), (trans_hbm.at[span],), more.at[slice(len(copies), len(copies) + 1)])
    arrive(copies)


def second_kernel(
    deep, middle_ref, gathered_ref, points_hbm, weights_hbm, drift_hbm, end_hbm, root_hbm, sent_ref,
    held, total, near, far, scaled, kept, sems, more, points_ref, weights_ref, drift_ref,
):
    arrivals = fetch((points_hbm, weights_hbm, drift_hbm), (points_ref, weights_ref, drift_ref), sems)
    size = points_ref.shape[1]
    early = end_hbm.shape[0]
    blocks = [(0, start) for start in range(0, early, BLOCK)] + [(1, start) for start in range(0, size, BLOCK)]
    copies = [
        pltpu.make_async_copy(
            (end_hbm, root_hbm)[half].at[start : start + BLOCK, :],
            kept.at[BLOCK * number : BLOCK * (number + 1), :],
            more.at[number],
        )
        for number, (half, start) in enumerate(blocks)
    ]
    for copy in copies[:AHEAD]:
        copy.start()
    chunks = middle_ref.shape[0]
    for chunk in range(chunks):
        columns = slice(chunk * LANES, (chunk + 1) * LANES)
        far[:, columns] = far_factor(gathered_ref[chunk, PAY:HALF, :].astype(F32)).astype(BF)
    arrive(arrivals)
    points = points_ref[...]
    rounded = points.astype(BF).astype(F32)
    late = points[:, early:]
    drift = row_of(drift_ref, late)
    near_factor(late, near_norms(late, weights_ref[:, early:], drift)[0], drift, held)
    near[...] = held[...].T.astype(BF)
    for half in range(2):
        rows = slice(PAY * (1 - half), PAY * (2 - half))
        for chunk in range(chunks):
            columns = slice(chunk * LANES, (chunk + 1) * LANES)
            pays = middle_ref[chunk, rows, :].astype(F32)
            for factor in range(FACTORS):
                scaled[half, PAY * factor : PAY * (factor + 1), columns] = (
                    pays * rounded[factor : factor + 1, columns]
                ).astype(BF)
            scaled[half, PAY * FACTORS :, columns] = pays.astype(BF)
    right = far[...]
    for start in range(early, size, deep):
        power = jnp.dot(near[start - early : start - early + deep, :], right, preferred_element_type=F32)
        trans = jnp.exp(power).astype(BF)
        part = jnp.dot(scaled[0, :, start : start + deep], trans, preferred_element_type=F32)
        total[0] = part if start == early else total[0] + part
    for number, (half, start) in enumerate(blocks):
        copies[number].wait()
        for copy in copies[number + AHEAD : number + AHEAD + 1]:
            copy.start()
        part = jnp.dot(
            scaled[half, :, start : start + BLOCK],
            kept[BLOCK * number : BLOCK * (number + 1), :],
            preferred_element_type=F32,
        )
        total[half] = part if half == 1 and start == 0 else total[half] + part
    for chunk in range(chunks):
        columns = slice(chunk * LANES, (chunk + 1) * LANES)
        grads = []
        for half in range(2):
            part = total[half, :, columns]
            block = gathered_ref[chunk, HALF * half : HALF * (half + 1), :].astype(F32)
            sides = weighted(block[:PAY], part)
            place = block[PAY : PAY + 4] + block[PAY + 4 : PAY + 8] + block[PAY + 8 : PAY + 12]
            for factor in range(FACTORS):
                rate = drift_ref[factor]
                spot = place[factor : factor + 1]
                if half == 0:
                    grads.append(rate * sides[factor] - spot * sides[FACTORS])
                else:
                    grads.append(rate * (sides[factor] - rate * spot * sides[FACTORS]))
        for row, grad in enumerate(grads):
            held[row : row + 1, 0:LANES] = grad
        sent_ref[chunk] = jnp.concatenate(
            [total[0, PAY * FACTORS :, columns], held[0 : 2 * FACTORS, 0:LANES]], axis=0
        ).astype(BF)


def last_kernel(got_ref, own_ref, terminal_ref, root_ref, mid_ref, end_ref):
    total = got_ref[0].astype(F32)
    own = own_ref[0]
    for device in range(1, got_ref.shape[0]):
        total = total + got_ref[device].astype(F32)
        own = own + own_ref[device]
    terminal_ref[...] = total[:PAY]
    end_ref[...] = total[PAY : PAY + FACTORS]
    root_ref[...] = total[PAY + FACTORS : PAY + 2 * FACTORS]
    mid_ref[...] = own


VMEM = pl.BlockSpec(memory_space=pltpu.VMEM)
HBM = pl.BlockSpec(memory_space=pltpu.HBM)
SMEM = pl.BlockSpec(memory_space=pltpu.SMEM)
PARAMS = pltpu.CompilerParams(vmem_limit_bytes=LIMIT)


def shape(dims, dtype):
    return jax.ShapeDtypeStruct(dims, dtype)


def held_back(*arrays):
    return [pltpu.with_memory_space_constraint(array, pltpu.HBM) for array in arrays]


def staged(*arrays):
    blocks = [pltpu.VMEM(array.shape, array.dtype) for array in arrays[:-1]]
    return blocks + [pltpu.SMEM(arrays[-1].shape, arrays[-1].dtype)]


def pack_call(count, *arrays):
    return pl.pallas_call(
        pack_kernel,
        out_shape=pltpu.HBM((count, 2 * HALF, LANES), BF),
        in_specs=[HBM] * 7,
        out_specs=VMEM,
        scratch_shapes=[pltpu.VMEM((2 * HALF, LANES), F32), pltpu.SemaphoreType.DMA((7,))]
        + staged(*arrays),
        compiler_params=PARAMS,
    )(*held_back(*arrays))


def near_call(points, weights, drift):
    size = points.shape[1]
    return pl.pallas_call(
        near_kernel,
        out_shape=(shape((2, DEPTH, size), BF), shape((2 * FACTORS, size), F32)),
        in_specs=[HBM] * 3,
        out_specs=(VMEM, VMEM),
        scratch_shapes=[pltpu.VMEM((DEPTH, size), F32), pltpu.SemaphoreType.DMA((3,))]
        + staged(points, weights, drift),
        compiler_params=PARAMS,
    )(*held_back(points, weights, drift))


def first_call(gathered, near, table):
    count, size = gathered.shape[0], near.shape[2]
    return pl.pallas_call(
        functools.partial(first_kernel, DEEP),
        out_shape=(
            pltpu.HBM((size // LANES, 2 * PAY, LANES), BF),
            pltpu.VMEM((2 * SIDES * PAY + 2 * FACTORS, size), F32),
        ),
        in_specs=[VMEM] * 3,
        out_specs=(VMEM, VMEM),
        scratch_shapes=[
            pltpu.VMEM((2, count * LANES, DEPTH), BF),
            pltpu.VMEM((2, SIDES * PAY, count * LANES), BF),
        ],
        compiler_params=PARAMS,
    )(gathered, near, table)


def middle_call(index, got, exercise, payoff, after):
    return pl.pallas_call(
        middle_kernel,
        out_shape=(pltpu.HBM(got.shape, BF), pltpu.HBM((8, LANES), F32)),
        in_specs=[SMEM, VMEM, HBM, HBM, HBM],
        out_specs=(VMEM, VMEM),
        scratch_shapes=[
            pltpu.SemaphoreType.DMA((2,)),
            pltpu.VMEM((PAY, LANES), jnp.int32),
            pltpu.VMEM((PAY, LANES), F32),
        ],
        compiler_params=PARAMS,
    )(index, got, *held_back(exercise, payoff, after))


def own_call(middle, sums):
    return pl.pallas_call(
        own_kernel,
        out_shape=pltpu.HBM((middle.shape[0], FACTORS, LANES), F32),
        in_specs=[VMEM] * 2,
        out_specs=VMEM,
        compiler_params=PARAMS,
    )(middle, sums)


def ahead_call(half, first, count, gathered, near, after):
    width = gathered.shape[0] * LANES
    return pl.pallas_call(
        functools.partial(ahead_kernel, half, first, DEEP),
        out_shape=pltpu.HBM((count, width), BF),
        in_specs=[VMEM, VMEM, HBM],
        out_specs=HBM,
        scratch_shapes=[
            pltpu.VMEM((count, DEPTH), BF),
            pltpu.VMEM((DEPTH, width), BF),
            pltpu.VMEM((count, width), BF),
            pltpu.SemaphoreType.DMA((count // PIECE,)),
        ],
        compiler_params=PARAMS,
        cost_estimate=pl.CostEstimate(
            flops=2 * 256 * count * width, bytes_accessed=2 * count * width, transcendentals=count * width
        ),
    )(gathered, near, *held_back(after))


def second_call(middle, gathered, points, weights, drift, end_trans, root_trans):
    count, size = gathered.shape[0], points.shape[1]
    width = count * LANES
    early = end_trans.shape[0]
    blocks = (early + size) // BLOCK
    return pl.pallas_call(
        functools.partial(second_kernel, DEEP),
        out_shape=shape((count, PAY + 2 * FACTORS, LANES), BF),
        in_specs=[VMEM] * 2 + [HBM] * 5,
        out_specs=VMEM,
        scratch_shapes=[
            pltpu.VMEM((DEPTH, size - early), F32),
            pltpu.VMEM((2, SIDES * PAY, width), F32),
            pltpu.VMEM((size - early, DEPTH), BF),
            pltpu.VMEM((DEPTH, width), BF),
            pltpu.VMEM((2, SIDES * PAY, size), BF),
            pltpu.VMEM((early + size, width), BF),
            pltpu.SemaphoreType.DMA((3,)),
            pltpu.SemaphoreType.DMA((blocks,)),
        ]
        + staged(points, weights, drift),
        compiler_params=PARAMS,
        cost_estimate=pl.CostEstimate(
            flops=4 * SIDES * PAY * size * size, bytes_accessed=4 * size * size, transcendentals=size * size
        ),
    )(middle, gathered, *held_back(points, weights, drift, end_trans, root_trans))


def last_call(got, own):
    return pl.pallas_call(
        last_kernel,
        out_shape=(shape((PAY, LANES), F32),) + (shape((FACTORS, LANES), F32),) * 3,
        in_specs=[VMEM] * 2,
        out_specs=(VMEM,) * 4,
        compiler_params=PARAMS,
    )(got, own)


def exchange(blocks, axis):
    return lax.all_to_all(blocks, axis, 0, 0)


def on_device(
    root_cot,
    root_exercise,
    mid_exercise,
    mid_payoff,
    end_values,
    root_points,
    mid_points,
    end_points,
    mid_weights,
    end_weights,
    drift_rate,
):
    rows = lax.axis_size("row")
    weights = mid_weights[None, :]
    packed = pack_call(
        rows, root_cot, root_exercise, end_values, root_points, end_points, end_weights[None, :], drift_rate
    )
    gathered = exchange(packed, "row")
    near, table = near_call(mid_points, weights, drift_rate)
    parts, sums = first_call(gathered, near, table)
    got = exchange(parts, "col")
    root_trans = ahead_call(1, 0, mid_points.shape[1], gathered, near, parts)
    values, mark = middle_call(lax.axis_index("col")[None], got, mid_exercise, mid_payoff, root_trans)
    middle = exchange(values, "col")
    end_trans = ahead_call(0, 0, EARLY, gathered, near, mark)
    own = exchange(own_call(middle, sums), "col")
    sides = second_call(middle, gathered, mid_points, weights, drift_rate, end_trans, root_trans)
    far = exchange(sides, "row")
    terminal, grad_root, grad_mid, grad_end = last_call(far, own)
    return (terminal, grad_root, grad_mid, grad_end)


def solution(mesh):
    in_specs = (
        P(None, ("col", "row")),
        P(None, ("col", "row")),
        P(None, "row"),
        P(None, "row"),
        P(None, ("col", "row")),
        P(None, ("col", "row")),
        P(None, "row"),
        P(None, ("col", "row")),
        P("row"),
        P(("col", "row")),
        P(),
    )
    out_specs = (
        P(None, ("col", "row")),
        P(None, ("col", "row")),
        P(None, ("row", "col")),
        P(None, ("col", "row")),
    )
    return jax.shard_map(
        on_device, mesh=mesh, in_specs=in_specs, out_specs=out_specs, check_vma=False
    )
```

```python
import functools

import jax
import jax.numpy as jnp
from jax import lax
from jax.experimental import pallas as pl
from jax.experimental.pallas import tpu as pltpu
from jax.sharding import PartitionSpec as P

BF = jnp.bfloat16
F32 = jnp.float32
LANES = 128
PAY = 32
FACTORS = 4
SIDES = FACTORS + 1
HALF = 48
DEPTH = 32
DEEP = 256
PIECE = 512
BLOCK = 1024
AHEAD = 2
EARLY = 1024
LIMIT = 36 * 1024 * 1024


def split3(value):
    high = value.astype(BF).astype(F32)
    rest = value - high
    middle = rest.astype(BF).astype(F32)
    return high, middle, (rest - middle).astype(BF).astype(F32)


def row_of(drift_ref, points):
    rows = lax.broadcasted_iota(jnp.int32, points.shape, 0)
    out = jnp.zeros(points.shape, F32)
    for factor in range(FACTORS):
        out = jnp.where(rows == factor, drift_ref[factor], out)
    return out


def square_sum(points):
    return jnp.sum(points * points, axis=0, keepdims=True)


def fetch(sources, places, sems):
    copies = [
        pltpu.make_async_copy(source, place, sems.at[number])
        for number, (source, place) in enumerate(zip(sources, places))
    ]
    for copy in copies:
        copy.start()
    return copies


def arrive(copies):
    for copy in copies:
        copy.wait()


def pack_kernel(
    cot_hbm, exercise_hbm, values_hbm, root_hbm, end_hbm, weight_hbm, drift_hbm, out_ref,
    held, sems, cot_ref, exercise_ref, values_ref, root_ref, end_ref, weight_ref, drift_ref,
):
    arrive(
        fetch(
            (cot_hbm, exercise_hbm, values_hbm, root_hbm, end_hbm, weight_hbm, drift_hbm),
            (cot_ref, exercise_ref, values_ref, root_ref, end_ref, weight_ref, drift_ref),
            sems,
        )
    )
    mask = 1.0 - exercise_ref[...].astype(F32)
    root = root_ref[...]
    end = end_ref[...]
    shifted = row_of(drift_ref, root) * root
    norms = (-0.5 * square_sum(end) + jnp.log(weight_ref[...]), -0.5 * square_sum(shifted))
    values = (values_ref[...].astype(F32), cot_ref[...].astype(F32) * mask)
    for half, (points, norm, pays) in enumerate(zip((end, root), norms, values)):
        base = HALF * half
        held[base : base + PAY, :] = pays
        for part, piece in enumerate(split3(points)):
            start = base + PAY + FACTORS * part
            held[start : start + FACTORS, :] = piece
        for part, piece in enumerate(split3(norm)):
            start = base + PAY + 3 * FACTORS + part
            held[start : start + 1, :] = piece
        held[base + HALF - 1 : base + HALF, :] = jnp.ones((1, LANES), F32)
    packed = held[...].astype(BF)
    for device in range(out_ref.shape[0]):
        out_ref[device] = packed


def far_factor(block):
    rows = lax.broadcasted_iota(jnp.int32, (8, block.shape[1]), 0)
    last = jnp.where(rows < FACTORS, block[0:8], jnp.where(rows < FACTORS + 2, 1.0, 0.0))
    return jnp.concatenate([block[0:8], block[0:8], block[8:16], last], axis=0)


def near_factor(points, norm, drift, held):
    high, middle, low = split3(drift * points)
    norms = split3(norm)
    ones = jnp.ones((3, points.shape[1]), F32)
    held[0:4, :] = high
    held[4:8, :] = high
    held[8:12, :] = middle
    held[12:16, :] = middle
    held[16:20, :] = high
    held[20:23, :] = ones
    held[23:24, :] = norms[0]
    held[24:28, :] = low
    held[28:29, :] = norms[1]
    held[29:30, :] = norms[2]
    held[30:32, :] = jnp.zeros((2, points.shape[1]), F32)


def near_norms(points, weights, drift):
    shifted = drift * points
    return (-0.5 * square_sum(shifted), -0.5 * square_sum(points) + jnp.log(weights))


def near_kernel(
    index_ref, points_hbm, weights_hbm, drift_hbm, exercise_hbm, payoff_hbm,
    near_ref, table_ref, chosen_ref, held, sems, points_ref, weights_ref, drift_ref, exercise_ref, payoff_ref,
):
    columns = pl.ds(pl.multiple_of(index_ref[0] * LANES, LANES), LANES)
    arrive(
        fetch(
            (points_hbm, weights_hbm, drift_hbm, exercise_hbm.at[:, columns], payoff_hbm.at[:, columns]),
            (points_ref, weights_ref, drift_ref, exercise_ref, payoff_ref),
            sems,
        )
    )
    mask = exercise_ref[...].astype(F32)
    chosen_ref[0:PAY, :] = mask * payoff_ref[...]
    chosen_ref[PAY:, :] = 1.0 - mask
    points = points_ref[...]
    drift = row_of(drift_ref, points)
    table_ref[0:FACTORS, :] = points
    table_ref[FACTORS:, :] = drift
    norms = near_norms(points, weights_ref[...], drift)
    for half in range(2):
        near_factor(points, norms[half], drift, held)
        near_ref[half] = held[...].astype(BF)


def first_kernel(deep, gathered_ref, near, table_ref, sent_ref, sums_ref, far, scaled):
    sums_ref[2 * SIDES * PAY :, :] = table_ref[...]
    chunks = gathered_ref.shape[0]
    for half in range(2):
        for chunk in range(chunks):
            columns = slice(chunk * LANES, (chunk + 1) * LANES)
            block = gathered_ref[chunk, HALF * half : HALF * (half + 1), :].astype(F32)
            pays, packed = block[:PAY], block[PAY:]
            far[half, columns, :] = far_factor(packed).T.astype(BF)
            for factor in range(FACTORS):
                scaled[half, PAY * factor : PAY * (factor + 1), columns] = (
                    pays * packed[factor : factor + 1]
                ).astype(BF)
            scaled[half, PAY * FACTORS :, columns] = pays.astype(BF)
    for half in range(2):
        right = near[half]
        for start in range(0, chunks * LANES, deep):
            rows = slice(start, start + deep)
            power = jnp.dot(far[half, rows, :], right, preferred_element_type=F32)
            trans = jnp.exp(power).astype(BF)
            part = jnp.dot(scaled[half, :, rows], trans, preferred_element_type=F32)
            place = slice(SIDES * PAY * half, SIDES * PAY * (half + 1))
            sums_ref[place, :] = part if start == 0 else sums_ref[place, :] + part
        last = sums_ref[SIDES * PAY * half + PAY * FACTORS : SIDES * PAY * (half + 1), :].astype(BF)
        for chunk in range(sent_ref.shape[0]):
            sent_ref[chunk, PAY * half : PAY * (half + 1), :] = last[
                :, chunk * LANES : (chunk + 1) * LANES
            ]


def middle_kernel(got_ref, chosen_ref, after_hbm, out_ref, mark_ref):
    total = got_ref[0].astype(F32)
    for device in range(1, got_ref.shape[0]):
        total = total + got_ref[device].astype(F32)
    live = chosen_ref[PAY:, :]
    values = chosen_ref[:PAY, :] + live * total[:PAY]
    packed = jnp.concatenate([values, live * total[PAY:]], axis=0).astype(BF)
    for device in range(out_ref.shape[0]):
        out_ref[device] = packed
    mark_ref[...] = values[0:8]


def weighted(pays, sums):
    return [
        jnp.sum(pays * sums[PAY * side : PAY * (side + 1)], axis=0, keepdims=True)
        for side in range(SIDES)
    ]


def own_kernel(middle_ref, sums_ref, own_ref):
    for chunk in range(middle_ref.shape[0]):
        columns = slice(chunk * LANES, (chunk + 1) * LANES)
        after = weighted(middle_ref[chunk, PAY:, :].astype(F32), sums_ref[: SIDES * PAY, columns])
        before = weighted(
            middle_ref[chunk, :PAY, :].astype(F32), sums_ref[SIDES * PAY : 2 * SIDES * PAY, columns]
        )
        for factor in range(FACTORS):
            row = 2 * SIDES * PAY + factor
            place = sums_ref[row : row + 1, columns]
            rate = sums_ref[row + FACTORS : row + FACTORS + 1, columns]
            own_ref[chunk, factor : factor + 1, :] = rate * (
                after[factor] - rate * place * after[FACTORS]
            ) - (place * before[FACTORS] - rate * before[factor])


def ahead_kernel(
    half, first, deep, gathered_ref, points_hbm, weights_hbm, drift_hbm, after_hbm, trans_hbm,
    held, near, far, kept, sems, points_ref, weights_ref, drift_ref, more,
):
    arrivals = fetch((points_hbm, weights_hbm, drift_hbm), (points_ref, weights_ref, drift_ref), sems)
    for chunk in range(gathered_ref.shape[0]):
        far[:, chunk * LANES : (chunk + 1) * LANES] = far_factor(
            gathered_ref[chunk, HALF * half + PAY : HALF * (half + 1), :].astype(F32)
        ).astype(BF)
    arrive(arrivals)
    count = kept.shape[0]
    points = points_ref[:, first : first + count]
    drift = row_of(drift_ref, points)
    near_factor(points, near_norms(points, weights_ref[:, first : first + count], drift)[half], drift, held)
    near[...] = held[...].T.astype(BF)
    right = far[...]
    copies = []
    for start in range(0, count, deep):
        rows = slice(start, start + deep)
        power = jnp.dot(near[rows, :], right, preferred_element_type=F32)
        kept[rows, :] = jnp.exp(power).astype(BF)
        if (start + deep) % PIECE == 0:
            span = slice(start + deep - PIECE, start + deep)
            copies += fetch((kept.at[span],), (trans_hbm.at[span],), more.at[slice(len(copies), len(copies) + 1)])
    arrive(copies)


def second_kernel(
    deep, middle_ref, gathered_ref, points_hbm, weights_hbm, drift_hbm, end_hbm, root_hbm, sent_ref,
    held, total, near, far, scaled, kept, sems, more, points_ref, weights_ref, drift_ref,
):
    arrivals = fetch((points_hbm, weights_hbm, drift_hbm), (points_ref, weights_ref, drift_ref), sems)
    size = points_ref.shape[1]
    early = end_hbm.shape[0]
    blocks = [(0, start) for start in range(0, early, BLOCK)] + [(1, start) for start in range(0, size, BLOCK)]
    copies = [
        pltpu.make_async_copy(
            (end_hbm, root_hbm)[half].at[start : start + BLOCK, :],
            kept.at[BLOCK * number : BLOCK * (number + 1), :],
            more.at[number],
        )
        for number, (half, start) in enumerate(blocks)
    ]
    for copy in copies[:AHEAD]:
        copy.start()
    chunks = middle_ref.shape[0]
    for chunk in range(chunks):
        columns = slice(chunk * LANES, (chunk + 1) * LANES)
        far[:, columns] = far_factor(gathered_ref[chunk, PAY:HALF, :].astype(F32)).astype(BF)
    arrive(arrivals)
    points = points_ref[...]
    rounded = points.astype(BF).astype(F32)
    late = points[:, early:]
    drift = row_of(drift_ref, late)
    near_factor(late, near_norms(late, weights_ref[:, early:], drift)[0], drift, held)
    near[...] = held[...].T.astype(BF)
    for half in range(2):
        rows = slice(PAY * (1 - half), PAY * (2 - half))
        for chunk in range(chunks):
            columns = slice(chunk * LANES, (chunk + 1) * LANES)
            pays = middle_ref[chunk, rows, :].astype(F32)
            for factor in range(FACTORS):
                scaled[half, PAY * factor : PAY * (factor + 1), columns] = (
                    pays * rounded[factor : factor + 1, columns]
                ).astype(BF)
            scaled[half, PAY * FACTORS :, columns] = pays.astype(BF)
    right = far[...]
    for start in range(early, size, deep):
        power = jnp.dot(near[start - early : start - early + deep, :], right, preferred_element_type=F32)
        trans = jnp.exp(power).astype(BF)
        part = jnp.dot(scaled[0, :, start : start + deep], trans, preferred_element_type=F32)
        total[0] = part if start == early else total[0] + part
    for number, (half, start) in enumerate(blocks):
        copies[number].wait()
        for copy in copies[number + AHEAD : number + AHEAD + 1]:
            copy.start()
        part = jnp.dot(
            scaled[half, :, start : start + BLOCK],
            kept[BLOCK * number : BLOCK * (number + 1), :],
            preferred_element_type=F32,
        )
        total[half] = part if half == 1 and start == 0 else total[half] + part
    for chunk in range(chunks):
        columns = slice(chunk * LANES, (chunk + 1) * LANES)
        grads = []
        for half in range(2):
            part = total[half, :, columns]
            block = gathered_ref[chunk, HALF * half : HALF * (half + 1), :].astype(F32)
            sides = weighted(block[:PAY], part)
            place = block[PAY : PAY + 4] + block[PAY + 4 : PAY + 8] + block[PAY + 8 : PAY + 12]
            for factor in range(FACTORS):
                rate = drift_ref[factor]
                spot = place[factor : factor + 1]
                if half == 0:
                    grads.append(rate * sides[factor] - spot * sides[FACTORS])
                else:
                    grads.append(rate * (sides[factor] - rate * spot * sides[FACTORS]))
        for row, grad in enumerate(grads):
            held[row : row + 1, 0:LANES] = grad
        sent_ref[chunk] = jnp.concatenate(
            [total[0, PAY * FACTORS :, columns], held[0 : 2 * FACTORS, 0:LANES]], axis=0
        ).astype(BF)


def last_kernel(got_ref, own_ref, terminal_ref, root_ref, mid_ref, end_ref):
    total = got_ref[0].astype(F32)
    own = own_ref[0]
    for device in range(1, got_ref.shape[0]):
        total = total + got_ref[device].astype(F32)
        own = own + own_ref[device]
    terminal_ref[...] = total[:PAY]
    end_ref[...] = total[PAY : PAY + FACTORS]
    root_ref[...] = total[PAY + FACTORS : PAY + 2 * FACTORS]
    mid_ref[...] = own


VMEM = pl.BlockSpec(memory_space=pltpu.VMEM)
HBM = pl.BlockSpec(memory_space=pltpu.HBM)
SMEM = pl.BlockSpec(memory_space=pltpu.SMEM)
PARAMS = pltpu.CompilerParams(vmem_limit_bytes=LIMIT)


def shape(dims, dtype):
    return jax.ShapeDtypeStruct(dims, dtype)


def held_back(*arrays):
    return [pltpu.with_memory_space_constraint(array, pltpu.HBM) for array in arrays]


def staged(*arrays):
    blocks = [pltpu.VMEM(array.shape, array.dtype) for array in arrays[:-1]]
    return blocks + [pltpu.SMEM(arrays[-1].shape, arrays[-1].dtype)]


def pack_call(count, *arrays):
    return pl.pallas_call(
        pack_kernel,
        out_shape=shape((count, 2 * HALF, LANES), BF),
        in_specs=[HBM] * 7,
        out_specs=VMEM,
        scratch_shapes=[pltpu.VMEM((2 * HALF, LANES), F32), pltpu.SemaphoreType.DMA((7,))]
        + staged(*arrays),
        compiler_params=PARAMS,
    )(*held_back(*arrays))


def near_call(index, points, weights, drift, exercise, payoff):
    size = points.shape[1]
    return pl.pallas_call(
        near_kernel,
        out_shape=(
            shape((2, DEPTH, size), BF),
            shape((2 * FACTORS, size), F32),
            shape((2 * PAY, LANES), F32),
        ),
        in_specs=[SMEM] + [HBM] * 5,
        out_specs=(VMEM, VMEM, VMEM),
        scratch_shapes=[pltpu.VMEM((DEPTH, size), F32), pltpu.SemaphoreType.DMA((5,))]
        + staged(points, weights, drift)
        + [pltpu.VMEM((PAY, LANES), jnp.int32), pltpu.VMEM((PAY, LANES), F32)],
        compiler_params=PARAMS,
    )(index, *held_back(points, weights, drift, exercise, payoff))


def first_call(gathered, near, table):
    count, size = gathered.shape[0], near.shape[2]
    return pl.pallas_call(
        functools.partial(first_kernel, DEEP),
        out_shape=(
            pltpu.HBM((size // LANES, 2 * PAY, LANES), BF),
            pltpu.VMEM((2 * SIDES * PAY + 2 * FACTORS, size), F32),
        ),
        in_specs=[VMEM] * 3,
        out_specs=(VMEM, VMEM),
        scratch_shapes=[
            pltpu.VMEM((2, count * LANES, DEPTH), BF),
            pltpu.VMEM((2, SIDES * PAY, count * LANES), BF),
        ],
        compiler_params=PARAMS,
    )(gathered, near, table)


def middle_call(got, chosen, after):
    return pl.pallas_call(
        middle_kernel,
        out_shape=(pltpu.HBM(got.shape, BF), pltpu.HBM((8, LANES), F32)),
        in_specs=[VMEM, VMEM, HBM],
        out_specs=(VMEM, VMEM),
        compiler_params=PARAMS,
    )(got, chosen, *held_back(after))


def own_call(middle, sums):
    return pl.pallas_call(
        own_kernel,
        out_shape=shape((middle.shape[0], FACTORS, LANES), F32),
        in_specs=[VMEM] * 2,
        out_specs=VMEM,
        compiler_params=PARAMS,
    )(middle, sums)


def ahead_call(half, first, count, gathered, points, weights, drift, after):
    size = points.shape[1]
    width = gathered.shape[0] * LANES
    return pl.pallas_call(
        functools.partial(ahead_kernel, half, first, DEEP),
        out_shape=pltpu.HBM((count, width), BF),
        in_specs=[VMEM] + [HBM] * 4,
        out_specs=HBM,
        scratch_shapes=[
            pltpu.VMEM((DEPTH, count), F32),
            pltpu.VMEM((count, DEPTH), BF),
            pltpu.VMEM((DEPTH, width), BF),
            pltpu.VMEM((count, width), BF),
            pltpu.SemaphoreType.DMA((3,)),
        ]
        + staged(points, weights, drift)
        + [pltpu.SemaphoreType.DMA((count // PIECE,))],
        compiler_params=PARAMS,
        cost_estimate=pl.CostEstimate(
            flops=2 * 256 * count * width, bytes_accessed=2 * count * width, transcendentals=count * width
        ),
    )(gathered, *held_back(points, weights, drift, after))


def second_call(middle, gathered, points, weights, drift, end_trans, root_trans):
    count, size = gathered.shape[0], points.shape[1]
    width = count * LANES
    early = end_trans.shape[0]
    blocks = (early + size) // BLOCK
    return pl.pallas_call(
        functools.partial(second_kernel, DEEP),
        out_shape=shape((count, PAY + 2 * FACTORS, LANES), BF),
        in_specs=[VMEM] * 2 + [HBM] * 5,
        out_specs=VMEM,
        scratch_shapes=[
            pltpu.VMEM((DEPTH, size - early), F32),
            pltpu.VMEM((2, SIDES * PAY, width), F32),
            pltpu.VMEM((size - early, DEPTH), BF),
            pltpu.VMEM((DEPTH, width), BF),
            pltpu.VMEM((2, SIDES * PAY, size), BF),
            pltpu.VMEM((early + size, width), BF),
            pltpu.SemaphoreType.DMA((3,)),
            pltpu.SemaphoreType.DMA((blocks,)),
        ]
        + staged(points, weights, drift),
        compiler_params=PARAMS,
        cost_estimate=pl.CostEstimate(
            flops=4 * SIDES * PAY * size * size, bytes_accessed=4 * size * size, transcendentals=size * size
        ),
    )(middle, gathered, *held_back(points, weights, drift, end_trans, root_trans))


def last_call(got, own):
    return pl.pallas_call(
        last_kernel,
        out_shape=(shape((PAY, LANES), F32),) + (shape((FACTORS, LANES), F32),) * 3,
        in_specs=[VMEM] * 2,
        out_specs=(VMEM,) * 4,
        compiler_params=PARAMS,
    )(got, own)


def exchange(blocks, axis):
    return lax.all_to_all(blocks, axis, 0, 0)


def on_device(
    root_cot,
    root_exercise,
    mid_exercise,
    mid_payoff,
    end_values,
    root_points,
    mid_points,
    end_points,
    mid_weights,
    end_weights,
    drift_rate,
):
    rows = lax.axis_size("row")
    weights = mid_weights[None, :]
    packed = pack_call(
        rows, root_cot, root_exercise, end_values, root_points, end_points, end_weights[None, :], drift_rate
    )
    gathered = exchange(packed, "row")
    index = lax.axis_index("col")[None]
    near, table, chosen = near_call(index, mid_points, weights, drift_rate, mid_exercise, mid_payoff)
    parts, sums = first_call(gathered, near, table)
    got = exchange(parts, "col")
    root_trans = ahead_call(1, 0, mid_points.shape[1], gathered, mid_points, weights, drift_rate, parts)
    values, mark = middle_call(got, chosen, root_trans)
    middle = exchange(values, "col")
    end_trans = ahead_call(0, 0, EARLY, gathered, mid_points, weights, drift_rate, mark)
    own = exchange(own_call(middle, sums), "col")
    sides = second_call(middle, gathered, mid_points, weights, drift_rate, end_trans, root_trans)
    far = exchange(sides, "row")
    terminal, grad_root, grad_mid, grad_end = last_call(far, own)
    return (terminal, grad_root, grad_mid, grad_end)


def solution(mesh):
    in_specs = (
        P(None, ("col", "row")),
        P(None, ("col", "row")),
        P(None, "row"),
        P(None, "row"),
        P(None, ("col", "row")),
        P(None, ("col", "row")),
        P(None, "row"),
        P(None, ("col", "row")),
        P("row"),
        P(("col", "row")),
        P(),
    )
    out_specs = (
        P(None, ("col", "row")),
        P(None, ("col", "row")),
        P(None, ("row", "col")),
        P(None, ("col", "row")),
    )
    return jax.shard_map(
        on_device, mesh=mesh, in_specs=in_specs, out_specs=out_specs, check_vma=False
    )
```

```python
import functools

import jax
import jax.numpy as jnp
from jax import lax
from jax.experimental import pallas as pl
from jax.experimental.pallas import tpu as pltpu
from jax.sharding import PartitionSpec as P

BF = jnp.bfloat16
F32 = jnp.float32
LANES = 128
PAY = 32
FACTORS = 4
SIDES = FACTORS + 1
ROWS = 88
DEPTH = 32
DEEP = 256
PIECE = 512
BLOCK = 1024
AHEAD = 2
EARLY = 1024
LIMIT = 36 * 1024 * 1024


def split2(value):
    high = value.astype(BF).astype(F32)
    return high, (value - high).astype(BF).astype(F32)


def split3(value):
    high, middle = split2(value)
    return high, middle, (value - high - middle).astype(BF).astype(F32)


def row_of(drift_ref, points):
    rows = lax.broadcasted_iota(jnp.int32, points.shape, 0)
    out = jnp.zeros(points.shape, F32)
    for factor in range(FACTORS):
        out = jnp.where(rows == factor, drift_ref[factor], out)
    return out


def square_sum(points):
    return jnp.sum(points * points, axis=0, keepdims=True)


def fetch(sources, places, sems):
    copies = [
        pltpu.make_async_copy(source, place, sems.at[number])
        for number, (source, place) in enumerate(zip(sources, places))
    ]
    for copy in copies:
        copy.start()
    return copies


def arrive(copies):
    for copy in copies:
        copy.wait()


def pack_kernel(
    cot_hbm, exercise_hbm, values_hbm, root_hbm, end_hbm, weight_hbm, drift_hbm, out_ref,
    held, sems, cot_ref, exercise_ref, values_ref, root_ref, end_ref, weight_ref, drift_ref,
):
    arrive(
        fetch(
            (cot_hbm, exercise_hbm, values_hbm, root_hbm, end_hbm, weight_hbm, drift_hbm),
            (cot_ref, exercise_ref, values_ref, root_ref, end_ref, weight_ref, drift_ref),
            sems,
        )
    )
    mask = 1.0 - exercise_ref[...].astype(F32)
    root = split2(root_ref[...])
    end = split2(end_ref[...])
    ends = end[0] + end[1]
    roots = root[0] + root[1]
    shifted = row_of(drift_ref, roots) * roots
    norms = (-0.5 * square_sum(ends) + jnp.log(weight_ref[...]), -0.5 * square_sum(shifted))
    held[0:PAY, :] = values_ref[...].astype(F32)
    held[PAY : 2 * PAY, :] = cot_ref[...].astype(F32) * mask
    for half, (parts, norm) in enumerate(zip((end, root), norms)):
        for part, piece in enumerate(parts):
            start = 2 * PAY + 8 * half + FACTORS * part
            held[start : start + FACTORS, :] = piece
        start = 2 * PAY + 16 + FACTORS * half
        for part, piece in enumerate(split3(norm)):
            held[start + part : start + part + 1, :] = piece
        held[start + 3 : start + 4, :] = jnp.ones((1, LANES), F32)
    packed = held[...].astype(BF)
    for device in range(out_ref.shape[0]):
        out_ref[device] = packed


def far_factor(half, points):
    width = points.shape[1]
    rows = lax.broadcasted_iota(jnp.int32, (8, width), 0)
    near_ones = (rows < 2) if half else (rows >= FACTORS) & (rows < FACTORS + 2)
    own = (rows >= FACTORS) if half else (rows < FACTORS)
    last = jnp.where(own, points[16:24], jnp.where(near_ones, 1.0, 0.0))
    both = points[8 * half : 8 * half + 8]
    return jnp.concatenate([both, both, last, jnp.zeros((8, width), F32)], axis=0)


def near_factor(points, weights, drift, held):
    high, middle = split2(drift * points)
    shifted = high + middle
    place = shifted / drift
    norms = (-0.5 * square_sum(shifted), -0.5 * square_sum(place) + jnp.log(weights))
    size = points.shape[1]
    for half in range(2):
        parts = split3(norms[half])
        held[half, 0:4, :] = high
        held[half, 4:8, :] = high
        held[half, 8:12, :] = middle
        held[half, 12:16, :] = middle
        base = 16 + FACTORS * half
        held[half, base : base + 3, :] = jnp.ones((3, size), F32)
        held[half, base + 3 : base + 4, :] = parts[0]
        base = 16 + FACTORS * (1 - half)
        held[half, base : base + 1, :] = parts[1]
        held[half, base + 1 : base + 2, :] = parts[2]
        held[half, base + 2 : base + 4, :] = jnp.zeros((2, size), F32)
        held[half, 24:32, :] = jnp.zeros((8, size), F32)


def near_kernel(
    index_ref, points_hbm, weights_hbm, drift_hbm, exercise_hbm, payoff_hbm,
    near_ref, table_ref, chosen_ref, held, sems, points_ref, weights_ref, drift_ref, exercise_ref, payoff_ref,
):
    columns = pl.ds(pl.multiple_of(index_ref[0] * LANES, LANES), LANES)
    arrive(
        fetch(
            (points_hbm, weights_hbm, drift_hbm, exercise_hbm.at[:, columns], payoff_hbm.at[:, columns]),
            (points_ref, weights_ref, drift_ref, exercise_ref, payoff_ref),
            sems,
        )
    )
    mask = exercise_ref[...].astype(F32)
    chosen_ref[0:PAY, :] = mask * payoff_ref[...]
    chosen_ref[PAY:, :] = 1.0 - mask
    points = points_ref[...]
    drift = row_of(drift_ref, points)
    table_ref[0:FACTORS, :] = points
    table_ref[FACTORS:, :] = drift
    near_factor(points, weights_ref[...], drift, held)
    near_ref[...] = held[...].astype(BF)


def first_kernel(deep, gathered_ref, near, table_ref, sent_ref, sums_ref, far, scaled):
    sums_ref[2 * SIDES * PAY :, :] = table_ref[...]
    chunks = gathered_ref.shape[0]
    for half in range(2):
        for chunk in range(chunks):
            columns = slice(chunk * LANES, (chunk + 1) * LANES)
            pays = gathered_ref[chunk, PAY * half : PAY * (half + 1), :].astype(F32)
            packed = gathered_ref[chunk, 2 * PAY :, :].astype(F32)
            far[half, columns, :] = far_factor(half, packed).T.astype(BF)
            for factor in range(FACTORS):
                scaled[half, PAY * factor : PAY * (factor + 1), columns] = (
                    pays * packed[8 * half + factor : 8 * half + factor + 1]
                ).astype(BF)
            scaled[half, PAY * FACTORS :, columns] = pays.astype(BF)
    for half in range(2):
        right = near[half]
        for start in range(0, chunks * LANES, deep):
            rows = slice(start, start + deep)
            power = jnp.dot(far[half, rows, :], right, preferred_element_type=F32)
            trans = jnp.exp(power).astype(BF)
            part = jnp.dot(scaled[half, :, rows], trans, preferred_element_type=F32)
            place = slice(SIDES * PAY * half, SIDES * PAY * (half + 1))
            sums_ref[place, :] = part if start == 0 else sums_ref[place, :] + part
        last = sums_ref[SIDES * PAY * half + PAY * FACTORS : SIDES * PAY * (half + 1), :].astype(BF)
        for chunk in range(sent_ref.shape[0]):
            sent_ref[chunk, PAY * half : PAY * (half + 1), :] = last[
                :, chunk * LANES : (chunk + 1) * LANES
            ]


def middle_kernel(got_ref, chosen_ref, after_hbm, out_ref, mark_ref):
    total = got_ref[0].astype(F32)
    for device in range(1, got_ref.shape[0]):
        total = total + got_ref[device].astype(F32)
    live = chosen_ref[PAY:, :]
    values = chosen_ref[:PAY, :] + live * total[:PAY]
    packed = jnp.concatenate([values, live * total[PAY:]], axis=0).astype(BF)
    for device in range(out_ref.shape[0]):
        out_ref[device] = packed
    mark_ref[...] = values[0:8]


def weighted(pays, sums):
    return [
        jnp.sum(pays * sums[PAY * side : PAY * (side + 1)], axis=0, keepdims=True)
        for side in range(SIDES)
    ]


def own_kernel(middle_ref, sums_ref, own_ref):
    for chunk in range(middle_ref.shape[0]):
        columns = slice(chunk * LANES, (chunk + 1) * LANES)
        after = weighted(middle_ref[chunk, PAY:, :].astype(F32), sums_ref[: SIDES * PAY, columns])
        before = weighted(
            middle_ref[chunk, :PAY, :].astype(F32), sums_ref[SIDES * PAY : 2 * SIDES * PAY, columns]
        )
        for factor in range(FACTORS):
            row = 2 * SIDES * PAY + factor
            place = sums_ref[row : row + 1, columns]
            rate = sums_ref[row + FACTORS : row + FACTORS + 1, columns]
            own_ref[chunk, factor : factor + 1, :] = rate * (
                after[factor] - rate * place * after[FACTORS]
            ) - (place * before[FACTORS] - rate * before[factor])


def ahead_kernel(
    half, first, deep, gathered_ref, points_hbm, weights_hbm, drift_hbm, after_hbm, trans_hbm,
    held, near, far, kept, sems, points_ref, weights_ref, drift_ref, more,
):
    arrivals = fetch((points_hbm, weights_hbm, drift_hbm), (points_ref, weights_ref, drift_ref), sems)
    for chunk in range(gathered_ref.shape[0]):
        far[:, chunk * LANES : (chunk + 1) * LANES] = far_factor(
            half, gathered_ref[chunk, 2 * PAY :, :].astype(F32)
        ).astype(BF)
    arrive(arrivals)
    count = kept.shape[0]
    points = points_ref[:, first : first + count]
    drift = row_of(drift_ref, points)
    near_factor(points, weights_ref[:, first : first + count], drift, held)
    near[...] = held[half].T.astype(BF)
    right = far[...]
    copies = []
    for start in range(0, count, deep):
        rows = slice(start, start + deep)
        power = jnp.dot(near[rows, :], right, preferred_element_type=F32)
        kept[rows, :] = jnp.exp(power).astype(BF)
        if (start + deep) % PIECE == 0:
            span = slice(start + deep - PIECE, start + deep)
            copies += fetch((kept.at[span],), (trans_hbm.at[span],), more.at[slice(len(copies), len(copies) + 1)])
    arrive(copies)


def second_kernel(
    deep, middle_ref, gathered_ref, points_hbm, weights_hbm, drift_hbm, end_hbm, root_hbm, sent_ref,
    held, total, near, far, scaled, kept, sems, more, points_ref, weights_ref, drift_ref,
):
    arrivals = fetch((points_hbm, weights_hbm, drift_hbm), (points_ref, weights_ref, drift_ref), sems)
    size = points_ref.shape[1]
    early = end_hbm.shape[0]
    blocks = [(0, start) for start in range(0, early, BLOCK)] + [(1, start) for start in range(0, size, BLOCK)]
    copies = [
        pltpu.make_async_copy(
            (end_hbm, root_hbm)[half].at[start : start + BLOCK, :],
            kept.at[BLOCK * number : BLOCK * (number + 1), :],
            more.at[number],
        )
        for number, (half, start) in enumerate(blocks)
    ]
    for copy in copies[:AHEAD]:
        copy.start()
    chunks = middle_ref.shape[0]
    for chunk in range(chunks):
        columns = slice(chunk * LANES, (chunk + 1) * LANES)
        far[:, columns] = far_factor(0, gathered_ref[chunk, 2 * PAY :, :].astype(F32)).astype(BF)
    arrive(arrivals)
    points = points_ref[...]
    rounded = points.astype(BF).astype(F32)
    late = points[:, early:]
    drift = row_of(drift_ref, late)
    near_factor(late, weights_ref[:, early:], drift, held)
    near[...] = held[0].T.astype(BF)
    for half in range(2):
        rows = slice(PAY * (1 - half), PAY * (2 - half))
        for chunk in range(chunks):
            columns = slice(chunk * LANES, (chunk + 1) * LANES)
            pays = middle_ref[chunk, rows, :].astype(F32)
            for factor in range(FACTORS):
                scaled[half, PAY * factor : PAY * (factor + 1), columns] = (
                    pays * rounded[factor : factor + 1, columns]
                ).astype(BF)
            scaled[half, PAY * FACTORS :, columns] = pays.astype(BF)
    right = far[...]
    for start in range(early, size, deep):
        power = jnp.dot(near[start - early : start - early + deep, :], right, preferred_element_type=F32)
        trans = jnp.exp(power).astype(BF)
        part = jnp.dot(scaled[0, :, start : start + deep], trans, preferred_element_type=F32)
        total[0] = part if start == early else total[0] + part
    for number, (half, start) in enumerate(blocks):
        copies[number].wait()
        for copy in copies[number + AHEAD : number + AHEAD + 1]:
            copy.start()
        part = jnp.dot(
            scaled[half, :, start : start + BLOCK],
            kept[BLOCK * number : BLOCK * (number + 1), :],
            preferred_element_type=F32,
        )
        total[half] = part if half == 1 and start == 0 else total[half] + part
    for chunk in range(chunks):
        columns = slice(chunk * LANES, (chunk + 1) * LANES)
        grads = []
        spots = gathered_ref[chunk, 2 * PAY :, :].astype(F32)
        for half in range(2):
            part = total[half, :, columns]
            sides = weighted(gathered_ref[chunk, PAY * half : PAY * (half + 1), :].astype(F32), part)
            place = spots[8 * half : 8 * half + 4] + spots[8 * half + 4 : 8 * half + 8]
            for factor in range(FACTORS):
                rate = drift_ref[factor]
                spot = place[factor : factor + 1]
                if half == 0:
                    grads.append(rate * sides[factor] - spot * sides[FACTORS])
                else:
                    grads.append(rate * (sides[factor] - rate * spot * sides[FACTORS]))
        for row, grad in enumerate(grads):
            held[0, row : row + 1, 0:LANES] = grad
        sent_ref[chunk] = jnp.concatenate(
            [total[0, PAY * FACTORS :, columns], held[0, 0 : 2 * FACTORS, 0:LANES]], axis=0
        ).astype(BF)


def last_kernel(got_ref, own_ref, terminal_ref, root_ref, mid_ref, end_ref):
    total = got_ref[0].astype(F32)
    own = own_ref[0]
    for device in range(1, got_ref.shape[0]):
        total = total + got_ref[device].astype(F32)
        own = own + own_ref[device]
    terminal_ref[...] = total[:PAY]
    end_ref[...] = total[PAY : PAY + FACTORS]
    root_ref[...] = total[PAY + FACTORS : PAY + 2 * FACTORS]
    mid_ref[...] = own


VMEM = pl.BlockSpec(memory_space=pltpu.VMEM)
HBM = pl.BlockSpec(memory_space=pltpu.HBM)
SMEM = pl.BlockSpec(memory_space=pltpu.SMEM)
PARAMS = pltpu.CompilerParams(vmem_limit_bytes=LIMIT)


def shape(dims, dtype):
    return jax.ShapeDtypeStruct(dims, dtype)


def held_back(*arrays):
    return [pltpu.with_memory_space_constraint(array, pltpu.HBM) for array in arrays]


def staged(*arrays):
    blocks = [pltpu.VMEM(array.shape, array.dtype) for array in arrays[:-1]]
    return blocks + [pltpu.SMEM(arrays[-1].shape, arrays[-1].dtype)]


def pack_call(count, *arrays):
    return pl.pallas_call(
        pack_kernel,
        out_shape=shape((count, ROWS, LANES), BF),
        in_specs=[HBM] * 7,
        out_specs=VMEM,
        scratch_shapes=[pltpu.VMEM((ROWS, LANES), F32), pltpu.SemaphoreType.DMA((7,))]
        + staged(*arrays),
        compiler_params=PARAMS,
    )(*held_back(*arrays))


def near_call(index, points, weights, drift, exercise, payoff):
    size = points.shape[1]
    return pl.pallas_call(
        near_kernel,
        out_shape=(
            shape((2, DEPTH, size), BF),
            shape((2 * FACTORS, size), F32),
            shape((2 * PAY, LANES), F32),
        ),
        in_specs=[SMEM] + [HBM] * 5,
        out_specs=(VMEM, VMEM, VMEM),
        scratch_shapes=[pltpu.VMEM((2, DEPTH, size), F32), pltpu.SemaphoreType.DMA((5,))]
        + staged(points, weights, drift)
        + [pltpu.VMEM((PAY, LANES), jnp.int32), pltpu.VMEM((PAY, LANES), F32)],
        compiler_params=PARAMS,
    )(index, *held_back(points, weights, drift, exercise, payoff))


def first_call(gathered, near, table):
    count, size = gathered.shape[0], near.shape[2]
    return pl.pallas_call(
        functools.partial(first_kernel, DEEP),
        out_shape=(
            pltpu.HBM((size // LANES, 2 * PAY, LANES), BF),
            pltpu.VMEM((2 * SIDES * PAY + 2 * FACTORS, size), F32),
        ),
        in_specs=[VMEM] * 3,
        out_specs=(VMEM, VMEM),
        scratch_shapes=[
            pltpu.VMEM((2, count * LANES, DEPTH), BF),
            pltpu.VMEM((2, SIDES * PAY, count * LANES), BF),
        ],
        compiler_params=PARAMS,
    )(gathered, near, table)


def middle_call(got, chosen, after):
    return pl.pallas_call(
        middle_kernel,
        out_shape=(pltpu.HBM(got.shape, BF), pltpu.HBM((8, LANES), F32)),
        in_specs=[VMEM, VMEM, HBM],
        out_specs=(VMEM, VMEM),
        compiler_params=PARAMS,
    )(got, chosen, *held_back(after))


def own_call(middle, sums):
    return pl.pallas_call(
        own_kernel,
        out_shape=shape((middle.shape[0], FACTORS, LANES), F32),
        in_specs=[VMEM] * 2,
        out_specs=VMEM,
        compiler_params=PARAMS,
    )(middle, sums)


def ahead_call(half, first, count, gathered, points, weights, drift, after):
    size = points.shape[1]
    width = gathered.shape[0] * LANES
    return pl.pallas_call(
        functools.partial(ahead_kernel, half, first, DEEP),
        out_shape=pltpu.HBM((count, width), BF),
        in_specs=[VMEM] + [HBM] * 4,
        out_specs=HBM,
        scratch_shapes=[
            pltpu.VMEM((2, DEPTH, count), F32),
            pltpu.VMEM((count, DEPTH), BF),
            pltpu.VMEM((DEPTH, width), BF),
            pltpu.VMEM((count, width), BF),
            pltpu.SemaphoreType.DMA((3,)),
        ]
        + staged(points, weights, drift)
        + [pltpu.SemaphoreType.DMA((count // PIECE,))],
        compiler_params=PARAMS,
        cost_estimate=pl.CostEstimate(
            flops=2 * 256 * count * width, bytes_accessed=2 * count * width, transcendentals=count * width
        ),
    )(gathered, *held_back(points, weights, drift, after))


def second_call(middle, gathered, points, weights, drift, end_trans, root_trans):
    count, size = gathered.shape[0], points.shape[1]
    width = count * LANES
    early = end_trans.shape[0]
    blocks = (early + size) // BLOCK
    return pl.pallas_call(
        functools.partial(second_kernel, DEEP),
        out_shape=shape((count, PAY + 2 * FACTORS, LANES), BF),
        in_specs=[VMEM] * 2 + [HBM] * 5,
        out_specs=VMEM,
        scratch_shapes=[
            pltpu.VMEM((2, DEPTH, size - early), F32),
            pltpu.VMEM((2, SIDES * PAY, width), F32),
            pltpu.VMEM((size - early, DEPTH), BF),
            pltpu.VMEM((DEPTH, width), BF),
            pltpu.VMEM((2, SIDES * PAY, size), BF),
            pltpu.VMEM((early + size, width), BF),
            pltpu.SemaphoreType.DMA((3,)),
            pltpu.SemaphoreType.DMA((blocks,)),
        ]
        + staged(points, weights, drift),
        compiler_params=PARAMS,
        cost_estimate=pl.CostEstimate(
            flops=4 * SIDES * PAY * size * size, bytes_accessed=4 * size * size, transcendentals=size * size
        ),
    )(middle, gathered, *held_back(points, weights, drift, end_trans, root_trans))


def last_call(got, own):
    return pl.pallas_call(
        last_kernel,
        out_shape=(shape((PAY, LANES), F32),) + (shape((FACTORS, LANES), F32),) * 3,
        in_specs=[VMEM] * 2,
        out_specs=(VMEM,) * 4,
        compiler_params=PARAMS,
    )(got, own)


def exchange(blocks, axis):
    return lax.all_to_all(blocks, axis, 0, 0)


def on_device(
    root_cot,
    root_exercise,
    mid_exercise,
    mid_payoff,
    end_values,
    root_points,
    mid_points,
    end_points,
    mid_weights,
    end_weights,
    drift_rate,
):
    rows = lax.axis_size("row")
    weights = mid_weights[None, :]
    packed = pack_call(
        rows, root_cot, root_exercise, end_values, root_points, end_points, end_weights[None, :], drift_rate
    )
    gathered = exchange(packed, "row")
    index = lax.axis_index("col")[None]
    near, table, chosen = near_call(index, mid_points, weights, drift_rate, mid_exercise, mid_payoff)
    parts, sums = first_call(gathered, near, table)
    got = exchange(parts, "col")
    root_trans = ahead_call(1, 0, mid_points.shape[1], gathered, mid_points, weights, drift_rate, parts)
    values, mark = middle_call(got, chosen, root_trans)
    middle = exchange(values, "col")
    end_trans = ahead_call(0, 0, EARLY, gathered, mid_points, weights, drift_rate, mark)
    own = exchange(own_call(middle, sums), "col")
    sides = second_call(middle, gathered, mid_points, weights, drift_rate, end_trans, root_trans)
    far = exchange(sides, "row")
    terminal, grad_root, grad_mid, grad_end = last_call(far, own)
    return (terminal, grad_root, grad_mid, grad_end)


def solution(mesh):
    in_specs = (
        P(None, ("col", "row")),
        P(None, ("col", "row")),
        P(None, "row"),
        P(None, "row"),
        P(None, ("col", "row")),
        P(None, ("col", "row")),
        P(None, "row"),
        P(None, ("col", "row")),
        P("row"),
        P(("col", "row")),
        P(),
    )
    out_specs = (
        P(None, ("col", "row")),
        P(None, ("col", "row")),
        P(None, ("row", "col")),
        P(None, ("col", "row")),
    )
    return jax.shard_map(
        on_device, mesh=mesh, in_specs=in_specs, out_specs=out_specs, check_vma=False
    )
```

```python
import functools

import jax
import jax.numpy as jnp
from jax import lax
from jax.experimental import pallas as pl
from jax.experimental.pallas import tpu as pltpu
from jax.sharding import PartitionSpec as P

BF = jnp.bfloat16
F32 = jnp.float32
LANES = 128
PAY = 32
FACTORS = 4
SIDES = FACTORS + 1
ROWS = 88
DEPTH = 32
DEEP = 256
PIECE = 512
BLOCK = 1024
AHEAD = 2
EARLY = 1024
LIMIT = 36 * 1024 * 1024


def split2(value):
    high = value.astype(BF).astype(F32)
    return high, (value - high).astype(BF).astype(F32)


def split3(value):
    high, middle = split2(value)
    return high, middle, (value - high - middle).astype(BF).astype(F32)


def row_of(drift_ref, points):
    rows = lax.broadcasted_iota(jnp.int32, points.shape, 0)
    out = jnp.zeros(points.shape, F32)
    for factor in range(FACTORS):
        out = jnp.where(rows == factor, drift_ref[factor], out)
    return out


def square_sum(points):
    return jnp.sum(points * points, axis=0, keepdims=True)


def fetch(sources, places, sems):
    copies = [
        pltpu.make_async_copy(source, place, sems.at[number])
        for number, (source, place) in enumerate(zip(sources, places))
    ]
    for copy in copies:
        copy.start()
    return copies


def arrive(copies):
    for copy in copies:
        copy.wait()


def pack_kernel(
    cot_hbm, exercise_hbm, values_hbm, root_hbm, end_hbm, weight_hbm, drift_hbm, out_ref,
    held, sems, cot_ref, exercise_ref, values_ref, root_ref, end_ref, weight_ref, drift_ref,
):
    arrive(
        fetch(
            (cot_hbm, exercise_hbm, values_hbm, root_hbm, end_hbm, weight_hbm, drift_hbm),
            (cot_ref, exercise_ref, values_ref, root_ref, end_ref, weight_ref, drift_ref),
            sems,
        )
    )
    mask = 1.0 - exercise_ref[...].astype(F32)
    root = split2(root_ref[...])
    end = split2(end_ref[...])
    ends = end[0] + end[1]
    roots = root[0] + root[1]
    shifted = row_of(drift_ref, roots) * roots
    norms = (-0.5 * square_sum(ends) + jnp.log(weight_ref[...]), -0.5 * square_sum(shifted))
    held[0:PAY, :] = values_ref[...].astype(F32)
    held[PAY : 2 * PAY, :] = cot_ref[...].astype(F32) * mask
    for half, (parts, norm) in enumerate(zip((end, root), norms)):
        for part, piece in enumerate(parts):
            start = 2 * PAY + 8 * half + FACTORS * part
            held[start : start + FACTORS, :] = piece
        start = 2 * PAY + 16 + FACTORS * half
        for part, piece in enumerate(split3(norm)):
            held[start + part : start + part + 1, :] = piece
        held[start + 3 : start + 4, :] = jnp.ones((1, LANES), F32)
    packed = held[...].astype(BF)
    for device in range(out_ref.shape[0]):
        out_ref[device] = packed


def far_factor(half, points):
    width = points.shape[1]
    rows = lax.broadcasted_iota(jnp.int32, (8, width), 0)
    near_ones = (rows < 2) if half else (rows >= FACTORS) & (rows < FACTORS + 2)
    own = (rows >= FACTORS) if half else (rows < FACTORS)
    last = jnp.where(own, points[16:24], jnp.where(near_ones, 1.0, 0.0))
    both = points[8 * half : 8 * half + 8]
    return jnp.concatenate([both, both, last, jnp.zeros((8, width), F32)], axis=0)


def near_factor(points, weights, drift, held):
    high, middle = split2(drift * points)
    shifted = high + middle
    place = shifted / drift
    norms = (-0.5 * square_sum(shifted), -0.5 * square_sum(place) + jnp.log(weights))
    size = points.shape[1]
    for half in range(2):
        parts = split3(norms[half])
        held[half, 0:4, :] = high
        held[half, 4:8, :] = high
        held[half, 8:12, :] = middle
        held[half, 12:16, :] = middle
        base = 16 + FACTORS * half
        held[half, base : base + 3, :] = jnp.ones((3, size), F32)
        held[half, base + 3 : base + 4, :] = parts[0]
        base = 16 + FACTORS * (1 - half)
        held[half, base : base + 1, :] = parts[1]
        held[half, base + 1 : base + 2, :] = parts[2]
        held[half, base + 2 : base + 4, :] = jnp.zeros((2, size), F32)
        held[half, 24:32, :] = jnp.zeros((8, size), F32)


def near_kernel(
    index_ref, points_hbm, weights_hbm, drift_hbm, exercise_hbm, payoff_hbm,
    near_ref, table_ref, chosen_ref, held, sems, points_ref, weights_ref, drift_ref, exercise_ref, payoff_ref,
):
    columns = pl.ds(pl.multiple_of(index_ref[0] * LANES, LANES), LANES)
    arrive(
        fetch(
            (points_hbm, weights_hbm, drift_hbm, exercise_hbm.at[:, columns], payoff_hbm.at[:, columns]),
            (points_ref, weights_ref, drift_ref, exercise_ref, payoff_ref),
            sems,
        )
    )
    mask = exercise_ref[...].astype(F32)
    chosen_ref[0:PAY, :] = mask * payoff_ref[...]
    chosen_ref[PAY:, :] = 1.0 - mask
    points = points_ref[...]
    drift = row_of(drift_ref, points)
    table_ref[0:FACTORS, :] = points
    table_ref[FACTORS:, :] = drift
    near_factor(points, weights_ref[...], drift, held)
    near_ref[...] = held[...].astype(BF)


def first_kernel(deep, gathered_ref, near, table_ref, sent_ref, sums_ref, far, scaled):
    sums_ref[2 * SIDES * PAY :, :] = table_ref[...]
    chunks = gathered_ref.shape[0]
    for half in range(2):
        for chunk in range(chunks):
            columns = slice(chunk * LANES, (chunk + 1) * LANES)
            pays = gathered_ref[chunk, PAY * half : PAY * (half + 1), :].astype(F32)
            packed = gathered_ref[chunk, 2 * PAY :, :].astype(F32)
            far[half, columns, :] = far_factor(half, packed).T.astype(BF)
            for factor in range(FACTORS):
                scaled[half, PAY * factor : PAY * (factor + 1), columns] = (
                    pays * packed[8 * half + factor : 8 * half + factor + 1]
                ).astype(BF)
            scaled[half, PAY * FACTORS :, columns] = pays.astype(BF)
        right = near[half]
        for start in range(0, chunks * LANES, deep):
            rows = slice(start, start + deep)
            power = jnp.dot(far[half, rows, :], right, preferred_element_type=F32)
            trans = jnp.exp(power).astype(BF)
            part = jnp.dot(scaled[half, :, rows], trans, preferred_element_type=F32)
            place = slice(SIDES * PAY * half, SIDES * PAY * (half + 1))
            sums_ref[place, :] = part if start == 0 else sums_ref[place, :] + part
        last = sums_ref[SIDES * PAY * half + PAY * FACTORS : SIDES * PAY * (half + 1), :].astype(BF)
        for chunk in range(sent_ref.shape[0]):
            sent_ref[chunk, PAY * half : PAY * (half + 1), :] = last[
                :, chunk * LANES : (chunk + 1) * LANES
            ]


def middle_kernel(got_ref, chosen_ref, after_hbm, out_ref, mark_ref):
    total = got_ref[0].astype(F32)
    for device in range(1, got_ref.shape[0]):
        total = total + got_ref[device].astype(F32)
    live = chosen_ref[PAY:, :]
    values = chosen_ref[:PAY, :] + live * total[:PAY]
    packed = jnp.concatenate([values, live * total[PAY:]], axis=0).astype(BF)
    for device in range(out_ref.shape[0]):
        out_ref[device] = packed
    mark_ref[...] = values[0:8]


def weighted(pays, sums):
    return [
        jnp.sum(pays * sums[PAY * side : PAY * (side + 1)], axis=0, keepdims=True)
        for side in range(SIDES)
    ]


def own_kernel(middle_ref, sums_ref, own_ref):
    for chunk in range(middle_ref.shape[0]):
        columns = slice(chunk * LANES, (chunk + 1) * LANES)
        after = weighted(middle_ref[chunk, PAY:, :].astype(F32), sums_ref[: SIDES * PAY, columns])
        before = weighted(
            middle_ref[chunk, :PAY, :].astype(F32), sums_ref[SIDES * PAY : 2 * SIDES * PAY, columns]
        )
        for factor in range(FACTORS):
            row = 2 * SIDES * PAY + factor
            place = sums_ref[row : row + 1, columns]
            rate = sums_ref[row + FACTORS : row + FACTORS + 1, columns]
            own_ref[chunk, factor : factor + 1, :] = rate * (
                after[factor] - rate * place * after[FACTORS]
            ) - (place * before[FACTORS] - rate * before[factor])


def ahead_kernel(
    half, first, deep, gathered_ref, points_hbm, weights_hbm, drift_hbm, after_hbm, trans_hbm,
    held, near, far, kept, sems, points_ref, weights_ref, drift_ref, more,
):
    arrivals = fetch((points_hbm, weights_hbm, drift_hbm), (points_ref, weights_ref, drift_ref), sems)
    for chunk in range(gathered_ref.shape[0]):
        far[:, chunk * LANES : (chunk + 1) * LANES] = far_factor(
            half, gathered_ref[chunk, 2 * PAY :, :].astype(F32)
        ).astype(BF)
    arrive(arrivals)
    count = kept.shape[0]
    points = points_ref[:, first : first + count]
    drift = row_of(drift_ref, points)
    near_factor(points, weights_ref[:, first : first + count], drift, held)
    near[...] = held[half].T.astype(BF)
    right = far[...]
    copies = []
    for start in range(0, count, deep):
        rows = slice(start, start + deep)
        power = jnp.dot(near[rows, :], right, preferred_element_type=F32)
        kept[rows, :] = jnp.exp(power).astype(BF)
        if (start + deep) % PIECE == 0:
            span = slice(start + deep - PIECE, start + deep)
            copies += fetch((kept.at[span],), (trans_hbm.at[span],), more.at[slice(len(copies), len(copies) + 1)])
    arrive(copies)


def second_kernel(
    deep, middle_ref, gathered_ref, points_hbm, weights_hbm, drift_hbm, end_hbm, root_hbm, sent_ref,
    held, total, near, far, scaled, kept, sems, more, points_ref, weights_ref, drift_ref,
):
    arrivals = fetch((points_hbm, weights_hbm, drift_hbm), (points_ref, weights_ref, drift_ref), sems)
    size = points_ref.shape[1]
    early = end_hbm.shape[0]
    blocks = [(0, start) for start in range(0, early, BLOCK)] + [(1, start) for start in range(0, size, BLOCK)]
    copies = [
        pltpu.make_async_copy(
            (end_hbm, root_hbm)[half].at[start : start + BLOCK, :],
            kept.at[BLOCK * number : BLOCK * (number + 1), :],
            more.at[number],
        )
        for number, (half, start) in enumerate(blocks)
    ]
    for copy in copies[:AHEAD]:
        copy.start()
    chunks = middle_ref.shape[0]
    for chunk in range(chunks):
        columns = slice(chunk * LANES, (chunk + 1) * LANES)
        far[:, columns] = far_factor(0, gathered_ref[chunk, 2 * PAY :, :].astype(F32)).astype(BF)
    arrive(arrivals)
    points = points_ref[...]
    rounded = points.astype(BF).astype(F32)
    late = points[:, early:]
    drift = row_of(drift_ref, late)
    near_factor(late, weights_ref[:, early:], drift, held)
    near[...] = held[0].T.astype(BF)
    def weigh(half):
        rows = slice(PAY * (1 - half), PAY * (2 - half))
        for chunk in range(chunks):
            columns = slice(chunk * LANES, (chunk + 1) * LANES)
            pays = middle_ref[chunk, rows, :].astype(F32)
            for factor in range(FACTORS):
                scaled[half, PAY * factor : PAY * (factor + 1), columns] = (
                    pays * rounded[factor : factor + 1, columns]
                ).astype(BF)
            scaled[half, PAY * FACTORS :, columns] = pays.astype(BF)
    weigh(0)
    right = far[...]
    for start in range(early, size, deep):
        power = jnp.dot(near[start - early : start - early + deep, :], right, preferred_element_type=F32)
        trans = jnp.exp(power).astype(BF)
        part = jnp.dot(scaled[0, :, start : start + deep], trans, preferred_element_type=F32)
        total[0] = part if start == early else total[0] + part
    weigh(1)
    for number, (half, start) in enumerate(blocks):
        copies[number].wait()
        for copy in copies[number + AHEAD : number + AHEAD + 1]:
            copy.start()
        part = jnp.dot(
            scaled[half, :, start : start + BLOCK],
            kept[BLOCK * number : BLOCK * (number + 1), :],
            preferred_element_type=F32,
        )
        total[half] = part if half == 1 and start == 0 else total[half] + part
    for chunk in range(chunks):
        columns = slice(chunk * LANES, (chunk + 1) * LANES)
        grads = []
        spots = gathered_ref[chunk, 2 * PAY :, :].astype(F32)
        for half in range(2):
            part = total[half, :, columns]
            sides = weighted(gathered_ref[chunk, PAY * half : PAY * (half + 1), :].astype(F32), part)
            place = spots[8 * half : 8 * half + 4] + spots[8 * half + 4 : 8 * half + 8]
            for factor in range(FACTORS):
                rate = drift_ref[factor]
                spot = place[factor : factor + 1]
                if half == 0:
                    grads.append(rate * sides[factor] - spot * sides[FACTORS])
                else:
                    grads.append(rate * (sides[factor] - rate * spot * sides[FACTORS]))
        for row, grad in enumerate(grads):
            held[0, row : row + 1, 0:LANES] = grad
        sent_ref[chunk] = jnp.concatenate(
            [total[0, PAY * FACTORS :, columns], held[0, 0 : 2 * FACTORS, 0:LANES]], axis=0
        ).astype(BF)


def last_kernel(got_ref, own_ref, terminal_ref, root_ref, mid_ref, end_ref):
    total = got_ref[0].astype(F32)
    own = own_ref[0]
    for device in range(1, got_ref.shape[0]):
        total = total + got_ref[device].astype(F32)
        own = own + own_ref[device]
    terminal_ref[...] = total[:PAY]
    end_ref[...] = total[PAY : PAY + FACTORS]
    root_ref[...] = total[PAY + FACTORS : PAY + 2 * FACTORS]
    mid_ref[...] = own


VMEM = pl.BlockSpec(memory_space=pltpu.VMEM)
HBM = pl.BlockSpec(memory_space=pltpu.HBM)
SMEM = pl.BlockSpec(memory_space=pltpu.SMEM)
PARAMS = pltpu.CompilerParams(vmem_limit_bytes=LIMIT)


def shape(dims, dtype):
    return jax.ShapeDtypeStruct(dims, dtype)


def held_back(*arrays):
    return [pltpu.with_memory_space_constraint(array, pltpu.HBM) for array in arrays]


def staged(*arrays):
    blocks = [pltpu.VMEM(array.shape, array.dtype) for array in arrays[:-1]]
    return blocks + [pltpu.SMEM(arrays[-1].shape, arrays[-1].dtype)]


def pack_call(count, *arrays):
    return pl.pallas_call(
        pack_kernel,
        out_shape=shape((count, ROWS, LANES), BF),
        in_specs=[HBM] * 7,
        out_specs=VMEM,
        scratch_shapes=[pltpu.VMEM((ROWS, LANES), F32), pltpu.SemaphoreType.DMA((7,))]
        + staged(*arrays),
        compiler_params=PARAMS,
    )(*held_back(*arrays))


def near_call(index, points, weights, drift, exercise, payoff):
    size = points.shape[1]
    return pl.pallas_call(
        near_kernel,
        out_shape=(
            shape((2, DEPTH, size), BF),
            shape((2 * FACTORS, size), F32),
            shape((2 * PAY, LANES), F32),
        ),
        in_specs=[SMEM] + [HBM] * 5,
        out_specs=(VMEM, VMEM, VMEM),
        scratch_shapes=[pltpu.VMEM((2, DEPTH, size), F32), pltpu.SemaphoreType.DMA((5,))]
        + staged(points, weights, drift)
        + [pltpu.VMEM((PAY, LANES), jnp.int32), pltpu.VMEM((PAY, LANES), F32)],
        compiler_params=PARAMS,
    )(index, *held_back(points, weights, drift, exercise, payoff))


def first_call(gathered, near, table):
    count, size = gathered.shape[0], near.shape[2]
    return pl.pallas_call(
        functools.partial(first_kernel, DEEP),
        out_shape=(
            pltpu.HBM((size // LANES, 2 * PAY, LANES), BF),
            pltpu.VMEM((2 * SIDES * PAY + 2 * FACTORS, size), F32),
        ),
        in_specs=[VMEM] * 3,
        out_specs=(VMEM, VMEM),
        scratch_shapes=[
            pltpu.VMEM((2, count * LANES, DEPTH), BF),
            pltpu.VMEM((2, SIDES * PAY, count * LANES), BF),
        ],
        compiler_params=PARAMS,
    )(gathered, near, table)


def middle_call(got, chosen, after):
    return pl.pallas_call(
        middle_kernel,
        out_shape=(pltpu.HBM(got.shape, BF), pltpu.HBM((8, LANES), F32)),
        in_specs=[VMEM, VMEM, HBM],
        out_specs=(VMEM, VMEM),
        compiler_params=PARAMS,
    )(got, chosen, *held_back(after))


def own_call(middle, sums):
    return pl.pallas_call(
        own_kernel,
        out_shape=shape((middle.shape[0], FACTORS, LANES), F32),
        in_specs=[VMEM] * 2,
        out_specs=VMEM,
        compiler_params=PARAMS,
    )(middle, sums)


def ahead_call(half, first, count, gathered, points, weights, drift, after):
    size = points.shape[1]
    width = gathered.shape[0] * LANES
    return pl.pallas_call(
        functools.partial(ahead_kernel, half, first, DEEP),
        out_shape=pltpu.HBM((count, width), BF),
        in_specs=[VMEM] + [HBM] * 4,
        out_specs=HBM,
        scratch_shapes=[
            pltpu.VMEM((2, DEPTH, count), F32),
            pltpu.VMEM((count, DEPTH), BF),
            pltpu.VMEM((DEPTH, width), BF),
            pltpu.VMEM((count, width), BF),
            pltpu.SemaphoreType.DMA((3,)),
        ]
        + staged(points, weights, drift)
        + [pltpu.SemaphoreType.DMA((count // PIECE,))],
        compiler_params=PARAMS,
        cost_estimate=pl.CostEstimate(
            flops=2 * 256 * count * width, bytes_accessed=2 * count * width, transcendentals=count * width
        ),
    )(gathered, *held_back(points, weights, drift, after))


def second_call(middle, gathered, points, weights, drift, end_trans, root_trans):
    count, size = gathered.shape[0], points.shape[1]
    width = count * LANES
    early = end_trans.shape[0]
    blocks = (early + size) // BLOCK
    return pl.pallas_call(
        functools.partial(second_kernel, DEEP),
        out_shape=shape((count, PAY + 2 * FACTORS, LANES), BF),
        in_specs=[VMEM] * 2 + [HBM] * 5,
        out_specs=VMEM,
        scratch_shapes=[
            pltpu.VMEM((2, DEPTH, size - early), F32),
            pltpu.VMEM((2, SIDES * PAY, width), F32),
            pltpu.VMEM((size - early, DEPTH), BF),
            pltpu.VMEM((DEPTH, width), BF),
            pltpu.VMEM((2, SIDES * PAY, size), BF),
            pltpu.VMEM((early + size, width), BF),
            pltpu.SemaphoreType.DMA((3,)),
            pltpu.SemaphoreType.DMA((blocks,)),
        ]
        + staged(points, weights, drift),
        compiler_params=PARAMS,
        cost_estimate=pl.CostEstimate(
            flops=4 * SIDES * PAY * size * size, bytes_accessed=4 * size * size, transcendentals=size * size
        ),
    )(middle, gathered, *held_back(points, weights, drift, end_trans, root_trans))


def last_call(got, own):
    return pl.pallas_call(
        last_kernel,
        out_shape=(shape((PAY, LANES), F32),) + (shape((FACTORS, LANES), F32),) * 3,
        in_specs=[VMEM] * 2,
        out_specs=(VMEM,) * 4,
        compiler_params=PARAMS,
    )(got, own)


def exchange(blocks, axis):
    return lax.all_to_all(blocks, axis, 0, 0)


def on_device(
    root_cot,
    root_exercise,
    mid_exercise,
    mid_payoff,
    end_values,
    root_points,
    mid_points,
    end_points,
    mid_weights,
    end_weights,
    drift_rate,
):
    rows = lax.axis_size("row")
    weights = mid_weights[None, :]
    packed = pack_call(
        rows, root_cot, root_exercise, end_values, root_points, end_points, end_weights[None, :], drift_rate
    )
    gathered = exchange(packed, "row")
    index = lax.axis_index("col")[None]
    near, table, chosen = near_call(index, mid_points, weights, drift_rate, mid_exercise, mid_payoff)
    parts, sums = first_call(gathered, near, table)
    got = exchange(parts, "col")
    root_trans = ahead_call(1, 0, mid_points.shape[1], gathered, mid_points, weights, drift_rate, parts)
    values, mark = middle_call(got, chosen, root_trans)
    middle = exchange(values, "col")
    end_trans = ahead_call(0, 0, EARLY, gathered, mid_points, weights, drift_rate, mark)
    own = exchange(own_call(middle, sums), "col")
    sides = second_call(middle, gathered, mid_points, weights, drift_rate, end_trans, root_trans)
    far = exchange(sides, "row")
    terminal, grad_root, grad_mid, grad_end = last_call(far, own)
    return (terminal, grad_root, grad_mid, grad_end)


def solution(mesh):
    in_specs = (
        P(None, ("col", "row")),
        P(None, ("col", "row")),
        P(None, "row"),
        P(None, "row"),
        P(None, ("col", "row")),
        P(None, ("col", "row")),
        P(None, "row"),
        P(None, ("col", "row")),
        P("row"),
        P(("col", "row")),
        P(),
    )
    out_specs = (
        P(None, ("col", "row")),
        P(None, ("col", "row")),
        P(None, ("row", "col")),
        P(None, ("col", "row")),
    )
    return jax.shard_map(
        on_device, mesh=mesh, in_specs=in_specs, out_specs=out_specs, check_vma=False
    )
```
